128 devices in a mesh: row: 16 (over y_lo, z, core), col: 8 (over y_hi, x).
Axes of the slice: x: 4, y: 4 (y_hi: 2, y_lo: 2; y = y_hi * 2 + y_lo), z: 4, core: 2. Of those that a mesh axis runs over, the one named last changes fastest.
Arguments:
- atom_single: bfloat16 [24576, 128], P(('row', 'col')), may hold values from -6 to 6
- pair_repr: bfloat16 [3072, 3072, 128], P('row', 'col'), may hold values from -384 to 384
- w_pair: bfloat16 [128, 4], replicated, may hold values from -0.5 to 0.5
- w_query: bfloat16 [128, 128], replicated, may hold values from -0.5 to 0.5
- w_keyval: bfloat16 [128, 256], replicated, may hold values from -0.5 to 0.5
- w_gate: bfloat16 [128, 128], replicated, may hold values from -0.5 to 0.5
- w_out: bfloat16 [128, 128], replicated, may hold values from -1.5 to 1.5
- w_agg: bfloat16 [128, 768], replicated, may hold values from -0.5 to 0.5
- atom_to_token: int32 [24576], P(('row', 'col')), may hold values from 0 to 3071, as said below
- window_shift: int32 [768], P(('row', 'col')), may hold values from -16 to 16
- atom_mask: int32 [24576], P(('row', 'col')), may hold values 0 or 1
Outputs:
- atoms: bfloat16 [24576, 128], P(('row', 'col'))
- token_single: bfloat16 [3072, 768], P('row', 'col')
The draws below stay inside these ranges and needn't reach their ends.
Inputs may be any that keep to these rules, and one draw needn't show every extreme that they name: `atom_to_token`: atom slots k * 192 to (k + 1) * 192 - 1 name tokens k * 24 to (k + 1) * 24 - 1 only; the list never falls and every token is named at least once.
All inputs are finite; a program needn't handle non-finite values. No bound on the sum of `atom_mask` on one device may be relied on, other than what follows from the above.
Results may differ from the reference program's by a relative error of at most 0.0069.
Values may be sent and summed in bfloat16 or wider, within the bound.
A program may use at most 128 MiB of HBM per device.

```python
import jax
import jax.numpy as jnp
from jax import lax

CA = 128
CZ = 128
CT = 768
HEADS = 4
QB = 32
KW = 128
TOK_DEV = 24
ATOM_DEV = 192
TOKENS = 3072
ATOMS = 24576
BLOCKS = 768


def draw_pair_repr(key, part):
    key = jax.random.fold_in(key, 11)
    shape = (TOKENS, TOKENS, CZ)
    base = jax.random.normal(key, shape, jnp.float32)
    return base.astype(jnp.bfloat16)


def draw_atom_to_token(key, part):
    key = jax.random.fold_in(key, 5)

    def one_block(index):
        sub = jax.random.fold_in(key, index)
        order = jax.random.permutation(sub, ATOM_DEV - 1)
        cuts = order[:TOK_DEV - 1] + 1
        marks = jnp.zeros((ATOM_DEV,), jnp.int32).at[cuts].set(1)
        return jnp.cumsum(marks).astype(jnp.int32) + index * TOK_DEV
    return jax.vmap(one_block)(jnp.arange(ATOMS // ATOM_DEV, dtype=jnp.int32)).reshape(-1)


def plant(values, own_key, least, top_value):
    longest = values.shape.index(max(values.shape))
    spots = []
    for shift in (0, 1):
        where = [jax.random.randint(jax.random.fold_in(own_key, axis), (), 0, length) for axis, length in enumerate(values.shape)]
        where[longest] = (where[longest] + shift) % values.shape[longest]
        spots.append(tuple(where))
    return values.at[spots[0]].set(least).at[spots[1]].set(top_value)


def block_scale(rng, extent, shards, low, largest):
    factor_of = 1.0
    for axis_at, parts in shards:
        steps = jax.random.uniform(jax.random.fold_in(jax.random.fold_in(rng, 6), axis_at), (parts,), jnp.float32, low / len(shards), largest / len(shards))
        factor_of = factor_of * jnp.repeat(jnp.exp(steps), extent[axis_at] // parts).reshape((-1,) + (1,) * (len(extent) - 1 - axis_at))
    return factor_of


def gaussian(key, dims, width, limit, pieces=(), kind=jnp.bfloat16):
    loudness = block_scale(key, dims, pieces, -0.22, 0.18) if pieces else 1.0
    result = jax.random.normal(key, dims, jnp.float32) * width * loudness
    return jnp.minimum(jnp.maximum(result, -limit), limit).astype(kind)


def setup_inputs(seed: int = 0) -> dict:
    seeds = jax.random.split(jax.random.key(seed), 12)
    return {
        "atom_single": gaussian(seeds[0], (ATOMS, CA), 1.0, 6.0, ((0, 128),)),
        "pair_repr": draw_pair_repr(jax.random.fold_in(seeds[11], 71), 0),
        "w_pair": gaussian(seeds[2], (CZ, HEADS), CZ ** -0.5, 0.5),
        "w_query": gaussian(seeds[3], (CA, CA), CA ** -0.5, 0.5),
        "w_keyval": gaussian(seeds[4], (CA, 2 * CA), CA ** -0.5, 0.5),
        "w_gate": gaussian(seeds[5], (CA, CA), CA ** -0.5, 0.5),
        "w_out": gaussian(seeds[6], (CA, CA), (CA // 8) ** -0.5, 1.5),
        "w_agg": gaussian(seeds[7], (CA, CT), CA ** -0.5, 0.5),
        "atom_to_token": draw_atom_to_token(jax.random.fold_in(seeds[11], 71), 0),
        "window_shift": plant(jax.random.randint(seeds[9], (BLOCKS,), 0 - QB // 2, QB // 2 + 1), jax.random.fold_in(seeds[9], 1), 0 - QB // 2, (QB // 2 + 1) - 1).astype(jnp.int32),
        "atom_mask": plant((jax.random.randint(seeds[10], (ATOMS,), 0, 8) < 7).astype(jnp.int32), jax.random.fold_in(seeds[10], 1), 0, 1),
    }


NEG = -1.0e9


def pair_table(pair_repr, w_pair):
    count = pair_repr.shape[0]
    stacked = pair_repr.reshape(count // TOK_DEV, TOK_DEV * count, CZ)

    def project(block):
        return jnp.dot(block, w_pair, preferred_element_type=jnp.float32)

    return lax.map(project, stacked).reshape(count, count, HEADS)


def reference(atom_single, pair_repr, w_pair, w_query, w_keyval, w_gate, w_out, w_agg, atom_to_token, window_shift, atom_mask):
    head_dim = CA // HEADS
    table = pair_table(pair_repr, w_pair)
    queries = jnp.dot(atom_single, w_query, preferred_element_type=jnp.float32).astype(jnp.bfloat16)
    keyval = jnp.dot(atom_single, w_keyval, preferred_element_type=jnp.float32).astype(jnp.bfloat16)
    gates = jax.nn.sigmoid(jnp.dot(atom_single, w_gate, preferred_element_type=jnp.float32))
    codes = jnp.where(atom_mask == 1, atom_to_token, -1).astype(jnp.int32)
    margin = KW // 2
    keyval_ext = jnp.pad(keyval, ((margin, margin), (0, 0)))
    codes_ext = jnp.pad(codes, (margin, margin), constant_values=-1)

    def attend(block):
        first = (block * QB).astype(jnp.int32)
        start = (first + QB // 2 + window_shift[block]).astype(jnp.int32)
        query_block = lax.dynamic_slice_in_dim(queries, first, QB, 0).astype(jnp.float32).reshape(QB, HEADS, head_dim)
        window = lax.dynamic_slice_in_dim(keyval_ext, start, KW, 0).astype(jnp.float32)
        key_codes = lax.dynamic_slice_in_dim(codes_ext, start, KW, 0)
        query_tokens = lax.dynamic_slice_in_dim(atom_to_token, first, QB, 0)
        bias = table[query_tokens[:, None], jnp.maximum(key_codes, 0)[None, :]]
        keys = window[:, :CA].reshape(KW, HEADS, head_dim)
        values = window[:, CA:].reshape(KW, HEADS, head_dim)
        scores = jnp.einsum("qhd,khd->hqk", query_block, keys, precision=lax.Precision.HIGHEST) * (head_dim ** -0.5)
        scores = scores + jnp.transpose(bias, (2, 0, 1))
        scores = jnp.where(key_codes[None, None, :] >= 0, scores, NEG)
        top = jnp.max(scores, axis=-1, keepdims=True)
        weights = jnp.exp(scores - top)
        probs = (weights / jnp.sum(weights, axis=-1, keepdims=True)).astype(jnp.bfloat16)
        mixed = jnp.einsum("hqk,khd->qhd", probs.astype(jnp.float32), values, precision=lax.Precision.HIGHEST).reshape(QB, CA)
        gate_block = lax.dynamic_slice_in_dim(gates, first, QB, 0)
        return (gate_block * mixed).astype(jnp.bfloat16)

    attended = lax.map(attend, jnp.arange(BLOCKS, dtype=jnp.int32)).reshape(ATOMS, CA)
    atoms = (atom_single.astype(jnp.float32) + jnp.dot(attended, w_out, preferred_element_type=jnp.float32)).astype(jnp.bfloat16)
    lifted = jax.nn.relu(jnp.dot(atoms, w_agg, preferred_element_type=jnp.float32)).astype(jnp.bfloat16)
    live = (atom_mask == 1).astype(jnp.float32)
    sums = jax.ops.segment_sum(lifted.astype(jnp.float32) * live[:, None], atom_to_token, num_segments=TOKENS)
    count = jax.ops.segment_sum(live, atom_to_token, num_segments=TOKENS)
    token_single = (sums / jnp.maximum(count, 1.0)[:, None]).astype(jnp.bfloat16)
    return atoms, token_single
```

```python
import functools
import math

import jax
import jax.numpy as jnp
from jax import lax
from jax.experimental import pallas as pl
from jax.experimental.pallas import tpu as pltpu
from jax.sharding import PartitionSpec as P

MESH = pl.DeviceIdType.MESH

QB = 32
KW = 128
WIDE = 80
SIDE = 48
OUTSIDE = -1.0e30
DEAD = -1.0e9
F32 = jnp.float32
BF16 = jnp.bfloat16


def dot(a, b):
    return jnp.dot(a, b, preferred_element_type=F32)


def dot_nt(a, b):
    return lax.dot_general(a, b, (((1,), (1,)), ((), ())), preferred_element_type=F32)


def kernel(
    n_row,
    n_col,
    x_in,
    pair_in,
    wp_in,
    wq_in,
    wkv_in,
    wg_in,
    wo_in,
    wa_in,
    tok_in,
    shift_in,
    mask_in,
    atoms_out,
    tok_recv,
    xs,
    strips,
    corner_x,
    wp,
    wq,
    wkv,
    wg,
    wo,
    wa,
    wa_pad,
    tok,
    mask,
    shift,
    tsend,
    csend,
    table,
    corner,
    messages,
    left_codes,
    right_codes,
    lhs,
    tok_send,
    in_sem,
    strip_sem,
    halo_send,
    halo_recv,
    table_send,
    table_recv,
    corner_send,
    corner_recv,
    tok_ssem,
    tok_rsem,
    ready,
    hello,
    go,
    corner_ready,
):
    row = lax.axis_index("row")
    col = lax.axis_index("col")
    me = row * n_col + col
    n_dev = n_row * n_col
    atoms = x_in.shape[0]
    width = x_in.shape[1]
    tok_rows, tok_cols, chan = pair_in.shape
    tok_dev = tok_rows // n_col
    half_t = tok_dev // 2
    heads = wp_in.shape[0]
    head_dim = width // heads
    margin = KW // 2
    per_col = tok_cols // tok_rows
    hold_col = row // per_col
    odd = row % per_col == per_col - 1
    even = row % per_col == 0
    is_holder = col == hold_col
    base = (row % per_col) * tok_rows

    def strip_start(j):
        want = base + tok_dev * (j - 1)
        want = jnp.maximum(want, 0)
        return jnp.minimum((want // 16) * 16, tok_cols - WIDE)

    has_left = me > 0
    has_right = me < n_dev - 1
    last = n_col - 1
    barrier = pltpu.get_barrier_semaphore()

    def edge(a, b):
        low = even & (b == hold_col - 1) & (a == 0)
        high = odd & (b == last) & (a == hold_col + 1)
        return (a != b) & ((a == hold_col) | (a == b - 1) | low | high)

    expected = jnp.where((col == last) & has_right, 1, 0)
    for other in range(n_col):
        expected = expected + jnp.where(edge(other, col), 1, 0)

        @pl.when(edge(col, other))
        def _():
            pl.semaphore_signal(barrier, inc=1, device_id=(row, other), device_id_type=MESH)

    @pl.when((col == 0) & has_left)
    def _():
        pl.semaphore_signal(barrier, inc=1, device_id=(row - 1, last), device_id_type=MESH)

    def local(i, src, dst):
        return pltpu.make_async_copy(src, dst, in_sem.at[i])

    wp_copy = local(0, wp_in, wp)
    x_copy = local(1, x_in, xs.at[pl.ds(0, atoms)])
    tok_copy = local(2, tok_in, tok)
    mask_copy = local(3, mask_in, mask)
    shift_copy = local(4, shift_in, shift)
    wkv_copy = local(5, wkv_in, wkv)
    wq_copy = local(6, wq_in, wq)
    wg_copy = local(7, wg_in, wg)
    wo_copy = local(8, wo_in, wo)
    wa_copy = local(9, wa_in, wa)
    wp_copy.start()

    def strip_copy(j):
        start = pl.multiple_of(strip_start(j), 16)
        return pltpu.make_async_copy(
            pair_in.at[pl.ds(tok_dev * j, tok_dev), pl.ds(start, WIDE)],
            strips.at[j],
            strip_sem.at[j],
        )

    x_copy.start()
    tok_copy.start()
    mask_copy.start()

    @pl.when(is_holder)
    def _():
        for j in range(n_col):
            strip_copy(j).start()

    shift_copy.start()
    wkv_copy.start()
    wq_copy.start()
    wg_copy.start()
    wo_copy.start()
    wa_copy.start()

    corner_to = jnp.where(even, 0, n_col - 1)
    give_even = even & (col == hold_col - 1)
    give_odd = odd & (col == hold_col + 1)
    gives_corner = give_even | give_odd
    takes_corner = (even & (row > 0) & (col == 0)) | (
        odd & (row < n_row - 1) & (col == n_col - 1)
    )
    corner_here = gives_corner & takes_corner
    corner_away = gives_corner & jnp.logical_not(takes_corner)
    corner_comes = takes_corner & jnp.logical_not(gives_corner)
    corner_col = pl.multiple_of(jnp.where(even, tok_cols - SIDE, 0), 16)
    corner_row = pl.multiple_of(jnp.where(even, 0, tok_rows - tok_dev), 8)
    corner_copy = pltpu.make_async_copy(
        pair_in.at[pl.ds(corner_row, tok_dev), pl.ds(corner_col, SIDE)], corner_x, in_sem.at[10]
    )

    @pl.when(gives_corner)
    def _():
        corner_copy.start()

    @pl.when(jnp.logical_not(corner_comes))
    def _():
        corner[...] = jnp.zeros_like(corner)

    left_id = (jnp.where(col > 0, row, row - 1), (col + n_col - 1) % n_col)
    right_id = (jnp.where(col < last, row, row + 1), (col + 1) % n_col)

    @pl.when(expected > 0)
    def _():
        pl.semaphore_wait(barrier, expected)

    @pl.when(jnp.logical_not(is_holder))
    def _():
        pl.semaphore_signal(
            ready.at[col], inc=1, device_id=(row, hold_col), device_id_type=MESH
        )

    @pl.when(col > 0)
    def _():
        pl.semaphore_signal(hello.at[0], inc=1, device_id=left_id, device_id_type=MESH)

    @pl.when((col == last) & has_right)
    def _():
        pl.semaphore_signal(hello.at[1], inc=1, device_id=right_id, device_id_type=MESH)

    corner_asks = corner_comes & odd

    @pl.when(corner_asks)
    def _():
        pl.semaphore_signal(
            corner_ready, inc=1, device_id=(row, hold_col + 1), device_id_type=MESH
        )

    wp_copy.wait()
    w_one = wp[...].astype(F32)
    w_rows = jnp.concatenate([w_one, w_one], axis=0)
    first_half = lax.broadcasted_iota(jnp.int32, w_rows.shape, 0) < heads
    w_both = jnp.concatenate(
        [jnp.where(first_half, w_rows, 0.0), jnp.where(first_half, 0.0, w_rows)], axis=1
    ).astype(BF16)

    def project(block):
        count = half_t * block.shape[1]
        low = block[:half_t].reshape(count, chan)
        high = block[half_t:].reshape(count, chan)
        return dot_nt(w_both, jnp.concatenate([low, high], axis=1))

    def corner_send_copy():
        return pltpu.make_async_remote_copy(
            src_ref=csend,
            dst_ref=corner,
            send_sem=corner_send,
            recv_sem=corner_recv,
            device_id=(row, corner_to),
            device_id_type=MESH,
        )

    def table_send_copy(j):
        return pltpu.make_async_remote_copy(
            src_ref=tsend.at[j],
            dst_ref=table,
            send_sem=table_send.at[j],
            recv_sem=table_recv,
            device_id=(row, j),
            device_id_type=MESH,
        )

    x_copy.wait()
    tok_copy.wait()
    mask_copy.wait()
    tokens = jnp.concatenate(
        [tok[...].reshape(1, atoms), jnp.full((1, 2 * width - atoms), -1, jnp.int32)], axis=1
    )
    masks = jnp.concatenate(
        [mask[...].reshape(1, atoms), jnp.zeros((1, 2 * width - atoms), jnp.int32)], axis=1
    )
    codes = jnp.where(masks == 1, tokens, -1)
    codes0, codes1 = codes[:, :width], codes[:, width:]
    messages[0] = jnp.broadcast_to(pltpu.roll(codes0, margin, 1), (8, width))
    messages[1] = jnp.broadcast_to(pltpu.roll(codes1, margin, 1), (8, width))

    def halo(i, src, dst, device):
        return pltpu.make_async_remote_copy(
            src_ref=src,
            dst_ref=dst,
            send_sem=halo_send.at[i],
            recv_sem=halo_recv.at[i],
            device_id=device,
            device_id_type=MESH,
        )

    to_left = (
        halo(0, xs.at[pl.ds(0, margin)], xs.at[pl.ds(atoms + margin, margin)], left_id),
        halo(1, messages.at[0], right_codes, left_id),
    )
    to_right = (
        halo(2, xs.at[pl.ds(atoms - margin, margin)], xs.at[pl.ds(atoms, margin)], right_id),
        halo(3, messages.at[1], left_codes, right_id),
    )

    @pl.when(jnp.logical_not(has_left))
    def _():
        xs[pl.ds(atoms, margin)] = jnp.zeros((margin, width), BF16)
        left_codes[...] = jnp.full(left_codes.shape, -1, jnp.int32)

    @pl.when(jnp.logical_not(has_right))
    def _():
        xs[pl.ds(atoms + margin, margin)] = jnp.zeros((margin, width), BF16)
        right_codes[...] = jnp.full(right_codes.shape, -1, jnp.int32)

    @pl.when(col > 0)
    def _():
        for copy in to_left:
            copy.start()

    @pl.when((col == last) & has_right)
    def _():
        for copy in to_right:
            copy.start()

    x_own = xs[pl.ds(0, atoms)]
    wq_copy.wait()
    queries = dot(x_own, wq[...])
    lanes = lax.broadcasted_iota(jnp.int32, (atoms, width), 1)
    local_tok = tokens - tok_dev * me
    upper = local_tok >= half_t
    place = jnp.where(upper, (local_tok - half_t) * 8 + heads, local_tok * 8)
    place = jnp.transpose(jnp.broadcast_to(place, (width, 2 * width)))[:atoms]
    first = atoms - margin
    for h in range(heads):
        q_h = jnp.where(lanes // head_dim == h, queries, 0.0).astype(BF16)
        hot_h = (lanes - h == place).astype(F32).astype(BF16)
        lhs[pl.ds(h * first, first), pl.ds(0, width)] = q_h[:first]
        lhs[pl.ds(h * first, first), pl.ds(width, width)] = hot_h[:first]
        lhs[pl.ds(heads * first + h * margin, margin), pl.ds(0, width)] = q_h[first:]
        lhs[pl.ds(heads * first + h * margin, margin), pl.ds(width, width)] = hot_h[first:]
    wg_copy.wait()
    gates = jax.nn.sigmoid(dot(x_own, wg[...]))
    wa_copy.wait()
    share = wa.shape[1] // n_col
    for c in range(n_col):
        part = jnp.concatenate(
            [wa[:, c * share : (c + 1) * share], jnp.zeros((width, width - share), BF16)], axis=1
        )
        wa_pad[:, c * width : (c + 1) * width] = part
    member = lax.broadcasted_iota(jnp.int32, (32, atoms), 0) == (codes - tok_dev * me)[:, :atoms]
    member = member.astype(F32)
    count = jnp.sum(member, axis=1, keepdims=True)
    inverse = 1.0 / jnp.maximum(count, 1.0)
    member = member.astype(BF16)

    group = n_col // 2

    @pl.when(is_holder)
    def _():
        for start in range(0, n_col, group):
            for j in range(start, start + group):
                strip_copy(j).wait()
            for j in range(start, start + group):
                tsend[j] = project(strips[j])
            for j in range(start, start + group):

                @pl.when(col != j)
                def _():
                    pl.semaphore_wait(ready.at[j], 1)
                    table_send_copy(j).start()

        for step in range(1, n_col):
            pl.semaphore_signal(
                go, inc=1, device_id=(row, (col + step) % n_col), device_id_type=MESH
            )
        table[...] = tsend[col]

    @pl.when(col < last)
    def _():
        pl.semaphore_wait(hello.at[0], 1)
        for copy in to_right:
            copy.start()

    @pl.when((col == 0) & has_left)
    def _():
        pl.semaphore_wait(hello.at[1], 1)
        for copy in to_left:
            copy.start()

    @pl.when(gives_corner)
    def _():
        corner_copy.wait()
        csend[...] = project(corner_x[...])

    @pl.when(corner_away & odd)
    def _():
        pl.semaphore_wait(corner_ready, 1)

    @pl.when(corner_away)
    def _():
        corner_send_copy().start()

    @pl.when(corner_here)
    def _():
        corner[...] = csend[...]

    @pl.when(has_left)
    def _():
        for copy in to_right:
            copy.wait_recv()

    @pl.when(has_right)
    def _():
        for copy in to_left:
            copy.wait_recv()

    wkv_copy.wait()
    keyval = dot(xs[...], wkv[...])
    keys_t = jnp.transpose(keyval[:, :width])
    keys_t = keys_t.astype(BF16)
    values = keyval[:, width:].astype(BF16)
    ones = jnp.ones((atoms + margin, width), BF16)
    v_a = jnp.concatenate([values[: atoms + margin], ones], axis=1)
    v_b = jnp.concatenate(
        [jnp.concatenate([values[:atoms], values[atoms + margin :]], axis=0), ones], axis=1
    )
    k_a = keys_t[:, : atoms + margin]
    k_b = jnp.concatenate([keys_t[:, :atoms], keys_t[:, atoms + margin :]], axis=1)
    side = lax.broadcasted_iota(jnp.int32, (1, width), 1)
    codes_a = jnp.where(side < margin, codes1, left_codes[0:1])
    codes_b = jnp.where(side < margin, codes1, right_codes[0:1])
    shift_copy.wait()
    lane2 = lax.broadcasted_iota(jnp.int32, (1, 2 * width), 1)
    at_a = jnp.where(lane2 < atoms, lane2, lane2 - 2 * width)
    full_a = jnp.concatenate([codes0, codes_a], axis=1)
    full_b = jnp.concatenate([codes0, codes_b], axis=1)
    caps = []
    for b in range(atoms // QB):
        start = QB * b - KW // 2 + QB // 2 + shift[b]
        at = at_a if b * QB < first else lane2
        code = full_a if b * QB < first else full_b
        inside = (at >= start) & (at < start + KW)
        cap = jnp.where(inside, jnp.where(code >= 0, 3.0e38, DEAD), OUTSIDE)
        caps.append(cap)

    @pl.when(jnp.logical_not(is_holder))
    def _():
        table_send_copy(0).wait_recv()

    @pl.when(corner_comes)
    def _():
        corner_send_copy().wait_recv()

    main = table[...]
    edge = corner[...]
    rows = [
        jnp.concatenate(
            [main[:, WIDE * t : WIDE * (t + 1)], edge[:, SIDE * t : SIDE * (t + 1)]], axis=1
        )
        for t in range(half_t)
    ]
    stacked = jnp.concatenate(rows, axis=0) * math.sqrt(head_dim)
    first_token = hold_col * tok_cols + strip_start(col)

    def spread(code):
        index = jnp.broadcast_to((code - first_token) & (width - 1), stacked.shape)
        return jnp.take_along_axis(stacked, index, axis=1, mode="promise_in_bounds")

    g_0, g_a, g_b = spread(codes0), spread(codes_a), spread(codes_b)
    pad_rows = jnp.zeros((width - stacked.shape[0], 2 * width), F32)

    def pieces(second):
        whole = jnp.concatenate([jnp.concatenate([g_0, second], axis=1), pad_rows], axis=0)
        high = whole.astype(BF16)
        rest = whole - high.astype(F32)
        mid = rest.astype(BF16)
        low = (rest - mid.astype(F32)).astype(BF16)
        return [high, mid, low]

    log_scale = math.log2(math.e) / math.sqrt(head_dim)

    def attend(first_row, n_rows, keys, second, vals, cap_list):
        both = lhs[pl.ds(first_row, heads * n_rows), :]
        hot = both[:, width:]
        left = jnp.concatenate([both, hot, hot], axis=1)
        right = jnp.concatenate([keys] + pieces(second), axis=0)
        scores = dot(left, right)
        parts = []
        per = n_rows // QB
        for i in range(heads * per):
            part = jnp.minimum(scores[i * QB : (i + 1) * QB], cap_list[i % per])
            top = jnp.max(part, axis=1, keepdims=True)
            parts.append(jnp.exp2((part - top) * log_scale).astype(BF16))
        weights = jnp.concatenate(parts, axis=0)
        mixed = dot(weights, vals)
        value, total = mixed[:n_rows, :width], mixed[:n_rows, width:]
        group = lax.broadcasted_iota(jnp.int32, (n_rows, width), 1) // head_dim
        for h in range(1, heads):
            value = jnp.where(group == h, mixed[h * n_rows : (h + 1) * n_rows, :width], value)
            total = jnp.where(group == h, mixed[h * n_rows : (h + 1) * n_rows, width:], total)
        return value / total

    n_a = first // QB
    out_a = attend(0, first, k_a, g_a, v_a, caps[:n_a])
    out_b = attend(heads * first, margin, k_b, g_b, v_b, caps[n_a:])
    attended = (gates * jnp.concatenate([out_a, out_b], axis=0)).astype(BF16)
    wo_copy.wait()
    new_atoms = (x_own.astype(F32) + dot(attended, wo[...])).astype(BF16)
    atoms_out[...] = new_atoms
    lifted = jnp.maximum(dot(new_atoms, wa_pad[...]), 0.0).astype(BF16)
    means = (dot(member, lifted) * inverse)[:tok_dev].astype(BF16)
    for c in range(n_col):
        tok_send[c] = means[:, c * width : (c + 1) * width]

    def tok_copy_to(step):
        other = (col + step) % n_col
        return pltpu.make_async_remote_copy(
            src_ref=tok_send.at[other],
            dst_ref=tok_recv.at[col],
            send_sem=tok_ssem.at[other],
            recv_sem=tok_rsem.at[col],
            device_id=(row, other),
            device_id_type=MESH,
        )

    def tok_copy_from(step):
        other = (col + step) % n_col
        return pltpu.make_async_remote_copy(
            src_ref=tok_send.at[other],
            dst_ref=tok_recv.at[other],
            send_sem=tok_ssem.at[other],
            recv_sem=tok_rsem.at[other],
            device_id=(row, other),
            device_id_type=MESH,
        )

    @pl.when(jnp.logical_not(is_holder))
    def _():
        pl.semaphore_wait(go, 1)

    for step in range(1, n_col):
        tok_copy_to(step).start()
    tok_recv[col] = tok_send[col]
    for step in range(1, n_col):
        tok_copy_from(step).wait_recv()

    for step in range(1, n_col):
        tok_copy_to(step).wait_send()

    @pl.when(is_holder)
    def _():
        for j in range(n_col):

            @pl.when(col != j)
            def _():
                table_send_copy(j).wait_send()

    @pl.when(corner_away)
    def _():
        corner_send_copy().wait_send()

    @pl.when(has_left)
    def _():
        for copy in to_left:
            copy.wait_send()

    @pl.when(has_right)
    def _():
        for copy in to_right:
            copy.wait_send()


def finish(atoms_ref, gathered, atoms_out, token_out, token_v, sems):
    atoms_copy = pltpu.make_async_copy(atoms_ref, atoms_out, sems.at[0])
    atoms_copy.start()
    rows = jnp.concatenate(
        [gathered[c].astype(F32) for c in range(gathered.shape[0])], axis=0
    )
    token_v[...] = rows.astype(BF16)[:, : token_v.shape[1]]
    token_copy = pltpu.make_async_copy(token_v, token_out, sems.at[1])
    token_copy.start()
    atoms_copy.wait()
    token_copy.wait()


def per_device(n_row, n_col, *args):
    x, pair, w_pair, w_query, w_keyval, w_gate, w_out, w_agg, tok, shift, mask = args
    w_pair = w_pair.T
    atoms, width = x.shape
    tok_rows, tok_cols, chan = pair.shape
    heads = w_pair.shape[0]
    tok_dev = tok_rows // n_col
    half_t = tok_dev // 2
    ct = w_agg.shape[1]
    margin = KW // 2
    hbm = pl.BlockSpec(memory_space=pltpu.HBM)
    vmem = pl.BlockSpec(memory_space=pltpu.VMEM)
    dma = pltpu.SemaphoreType.DMA
    regular = pltpu.SemaphoreType.REGULAR
    scratch = [
        pltpu.VMEM((atoms + 2 * margin, width), BF16),
        pltpu.VMEM((n_col, tok_dev, WIDE, chan), BF16),
        pltpu.VMEM((tok_dev, SIDE, chan), BF16),
        pltpu.VMEM(w_pair.shape, BF16),
        pltpu.VMEM(w_query.shape, BF16),
        pltpu.VMEM(w_keyval.shape, BF16),
        pltpu.VMEM(w_gate.shape, BF16),
        pltpu.VMEM(w_out.shape, BF16),
        pltpu.VMEM(w_agg.shape, BF16),
        pltpu.VMEM((width, n_col * width), BF16),
        pltpu.VMEM(tok.shape, jnp.int32),
        pltpu.VMEM(mask.shape, jnp.int32),
        pltpu.SMEM(shift.shape, jnp.int32),
        pltpu.VMEM((n_col, 2 * heads, half_t * WIDE), F32),
        pltpu.VMEM((2 * heads, half_t * SIDE), F32),
        pltpu.VMEM((2 * heads, half_t * WIDE), F32),
        pltpu.VMEM((2 * heads, half_t * SIDE), F32),
        pltpu.VMEM((2, 8, width), jnp.int32),
        pltpu.VMEM((8, width), jnp.int32),
        pltpu.VMEM((8, width), jnp.int32),
        pltpu.VMEM((heads * atoms, 2 * width), BF16),
        pltpu.VMEM((n_col, tok_dev, width), BF16),
        dma((11,)),
        dma((n_col,)),
        dma((4,)),
        dma((4,)),
        dma((n_col,)),
        dma,
        dma,
        dma,
        dma((n_col,)),
        dma((n_col,)),
        regular((n_col,)),
        regular((2,)),
        regular,
        regular,
    ]
    inputs = (x, pair, w_pair, w_query, w_keyval, w_gate, w_out, w_agg, tok, shift, mask)
    inputs = [pltpu.with_memory_space_constraint(a, pltpu.HBM) for a in inputs]
    new_atoms, gathered = pl.pallas_call(
        functools.partial(kernel, n_row, n_col),
        out_shape=(
            pltpu.VMEM((atoms, width), BF16),
            pltpu.VMEM((n_col, tok_dev, width), BF16),
        ),
        in_specs=[hbm] * 11,
        out_specs=(vmem, vmem),
        scratch_shapes=scratch,
        compiler_params=pltpu.CompilerParams(
            collective_id=0, has_side_effects=True, vmem_limit_bytes=40 * 1024 * 1024
        ),
        name="atom_block",
    )(*inputs)
    return pl.pallas_call(
        finish,
        out_shape=(
            pltpu.HBM((atoms, width), BF16),
            pltpu.HBM((tok_rows, ct // n_col), BF16),
        ),
        in_specs=[vmem, vmem],
        out_specs=(hbm, hbm),
        scratch_shapes=[pltpu.VMEM((tok_rows, ct // n_col), BF16), dma((2,))],
        compiler_params=pltpu.CompilerParams(vmem_limit_bytes=8 * 1024 * 1024),
        name="write_out",
    )(new_atoms, gathered)


def solution(mesh):
    n_row, n_col = mesh.shape["row"], mesh.shape["col"]
    split = P(("row", "col"))
    in_specs = (
        P(("row", "col"), None),
        P("row", "col", None),
        P(),
        P(),
        P(),
        P(),
        P(),
        P(),
        split,
        split,
        split,
    )
    out_specs = (P(("row", "col"), None), P("row", "col"))
    return jax.shard_map(
        functools.partial(per_device, n_row, n_col),
        mesh=mesh,
        in_specs=in_specs,
        out_specs=out_specs,
        check_vma=False,
    )
```

```python
import functools
import math

import jax
import jax.numpy as jnp
from jax import lax
from jax.experimental import pallas as pl
from jax.experimental.pallas import tpu as pltpu
from jax.sharding import PartitionSpec as P

MESH = pl.DeviceIdType.MESH

QB = 32
KW = 128
WIDE = 80
SIDE = 48
OUTSIDE = -(2.0**126)
DEAD = -(2.0**100)
F32 = jnp.float32
BF16 = jnp.bfloat16


def dot(a, b):
    return jnp.dot(a, b, preferred_element_type=F32)


def dot_nt(a, b):
    return lax.dot_general(a, b, (((1,), (1,)), ((), ())), preferred_element_type=F32)


def kernel(
    n_row,
    n_col,
    x_in,
    pair_in,
    wp_in,
    wq_in,
    wkv_in,
    wg_in,
    wo_in,
    wa_in,
    tok_in,
    shift_in,
    mask_in,
    atoms_out,
    tok_recv,
    xs,
    strips,
    corner_x,
    wp,
    wq,
    wkv,
    wg,
    wo,
    wa,
    tok,
    mask,
    shift,
    tsend,
    csend,
    table,
    corner,
    messages,
    codes_s,
    lhs,
    rhs,
    vals,
    tok_send,
    in_sem,
    strip_sem,
    halo_send,
    halo_recv,
    table_send,
    table_recv,
    corner_send,
    corner_recv,
    tok_ssem,
    tok_rsem,
):
    row = lax.axis_index("row")
    col = lax.axis_index("col")
    me = row * n_col + col
    n_dev = n_row * n_col
    atoms, width = x_in.shape
    tok_rows, tok_cols, chan = pair_in.shape
    tok_dev = tok_rows // n_col
    half_t = tok_dev // 2
    heads = wp_in.shape[0]
    head_dim = width // heads
    margin = KW // 2
    per_col = tok_cols // tok_rows
    hold_col = row // per_col
    odd = row % per_col == per_col - 1
    even = row % per_col == 0
    is_holder = col == hold_col
    base = (row % per_col) * tok_rows
    has_left = me > 0
    has_right = me < n_dev - 1

    def strip_start(j):
        want = jnp.maximum(base + tok_dev * (j - 1), 0)
        return jnp.minimum((want // 16) * 16, tok_cols - WIDE)

    barrier = pltpu.get_barrier_semaphore()

    for step in range(1, n_col):
        other = (col + step) % n_col
        pl.semaphore_signal(barrier, inc=1, device_id=(row, other), device_id_type=MESH)

    up_row = (col == 0) & has_left
    down_row = (col == n_col - 1) & has_right
    left_id = (jnp.where(col > 0, row, row - 1), (col + n_col - 1) % n_col)
    right_id = (jnp.where(col < n_col - 1, row, row + 1), (col + 1) % n_col)

    @pl.when(up_row)
    def _():
        pl.semaphore_signal(barrier, inc=1, device_id=left_id, device_id_type=MESH)

    @pl.when(down_row)
    def _():
        pl.semaphore_signal(barrier, inc=1, device_id=right_id, device_id_type=MESH)

    expected = n_col - 1 + up_row.astype(jnp.int32) + down_row.astype(jnp.int32)

    def local(i, src, dst):
        return pltpu.make_async_copy(src, dst, in_sem.at[i])

    tail = atoms - margin
    x_copy = local(0, x_in, xs.at[pl.ds(0, atoms)])
    tail_copy = local(1, x_in.at[pl.ds(tail, margin)], xs.at[pl.ds(2 * width, margin)])
    toks_copy = local(2, tok_in, tok)
    mask_copy = local(3, mask_in, mask)
    wp_copy = local(4, wp_in, wp)
    wq_copy = local(5, wq_in, wq)
    wg_copy = local(6, wg_in, wg)
    wkv_copy = local(7, wkv_in, wkv)
    shift_copy = local(8, shift_in, shift)
    wo_copy = local(9, wo_in, wo)
    wa_copy = local(10, wa_in, wa)

    def strip_copy(s):
        j = (col + 1 + s) % n_col
        start = pl.multiple_of(strip_start(j), 16)
        return pltpu.make_async_copy(
            pair_in.at[pl.ds(pl.multiple_of(tok_dev * j, 8), tok_dev), pl.ds(start, WIDE)],
            strips.at[s],
            strip_sem.at[s],
        )

    x_copy.start()
    toks_copy.start()
    mask_copy.start()
    wp_copy.start()

    @pl.when(is_holder)
    def _():
        for s in range(n_col):
            strip_copy(s).start()

    wq_copy.start()
    wg_copy.start()
    tail_copy.start()
    wkv_copy.start()
    shift_copy.start()
    wo_copy.start()
    wa_copy.start()

    corner_to = jnp.where(even, 0, n_col - 1)
    gives_corner = (even & (col == hold_col - 1)) | (odd & (col == hold_col + 1))
    takes_corner = (up_row & even) | (down_row & odd)
    corner_comes = takes_corner & jnp.logical_not(gives_corner)
    corner_away = gives_corner & jnp.logical_not(takes_corner)
    corner_col = pl.multiple_of(jnp.where(even, tok_cols - SIDE, 0), 16)
    corner_row = pl.multiple_of(jnp.where(even, 0, tok_rows - tok_dev), 8)
    corner_copy = pltpu.make_async_copy(
        pair_in.at[pl.ds(corner_row, tok_dev), pl.ds(corner_col, SIDE)], corner_x, in_sem.at[11]
    )

    @pl.when(gives_corner)
    def _():
        corner_copy.start()

    @pl.when(jnp.logical_not(corner_comes))
    def _():
        corner[...] = jnp.zeros_like(corner)

    def project(block):
        w_one = wp[...].astype(F32)
        w_rows = jnp.concatenate([w_one, w_one], axis=0)
        first_half = lax.broadcasted_iota(jnp.int32, w_rows.shape, 0) < heads
        w_both = jnp.concatenate(
            [jnp.where(first_half, w_rows, 0.0), jnp.where(first_half, 0.0, w_rows)], axis=1
        ).astype(BF16)
        count = half_t * block.shape[1]
        low = block[:half_t].reshape(count, chan)
        high = block[half_t:].reshape(count, chan)
        return dot_nt(w_both, jnp.concatenate([low, high], axis=1))

    def corner_send_copy():
        return pltpu.make_async_remote_copy(
            src_ref=csend,
            dst_ref=corner,
            send_sem=corner_send,
            recv_sem=corner_recv,
            device_id=(row, corner_to),
            device_id_type=MESH,
        )

    def table_send_copy(s):
        j = (col + 1 + s) % n_col
        return pltpu.make_async_remote_copy(
            src_ref=tsend.at[s],
            dst_ref=table,
            send_sem=table_send,
            recv_sem=table_recv,
            device_id=(row, j),
            device_id_type=MESH,
        )

    toks_copy.wait()
    mask_copy.wait()
    spare = 2 * width - atoms
    tokens = jnp.concatenate(
        [tok[...].reshape(1, atoms), jnp.full((1, spare), -1, jnp.int32)], axis=1
    )
    masks = jnp.concatenate(
        [mask[...].reshape(1, atoms), jnp.zeros((1, spare), jnp.int32)], axis=1
    )
    codes = jnp.where(masks == 1, tokens, -1)
    codes0, codes1 = codes[:, :width], codes[:, width:]
    messages[0] = jnp.broadcast_to(pltpu.roll(codes0, margin, 1), (8, width))
    messages[1] = jnp.broadcast_to(pltpu.roll(codes1, margin, 1), (8, width))

    def halo(i, src, dst, device):
        return pltpu.make_async_remote_copy(
            src_ref=src,
            dst_ref=dst,
            send_sem=halo_send.at[i],
            recv_sem=halo_recv.at[i],
            device_id=device,
            device_id_type=MESH,
        )

    x_left, x_right = pl.ds(atoms, margin), pl.ds(2 * width + margin, margin)
    to_left = (
        halo(0, xs.at[pl.ds(0, margin)], xs.at[x_right], left_id),
        halo(1, messages.at[0], codes_s.at[2], left_id),
    )
    to_right = (
        halo(2, xs.at[pl.ds(tail, margin)], xs.at[x_left], right_id),
        halo(3, messages.at[1], codes_s.at[1], right_id),
    )

    @pl.when(jnp.logical_not(has_left))
    def _():
        xs[x_left] = jnp.zeros((margin, width), BF16)
        codes_s[1] = jnp.full((8, width), -1, jnp.int32)

    @pl.when(jnp.logical_not(has_right))
    def _():
        xs[x_right] = jnp.zeros((margin, width), BF16)
        codes_s[2] = jnp.full((8, width), -1, jnp.int32)

    wp_copy.wait()
    group = n_col // 2

    @pl.when(is_holder)
    def _():
        for first in range(0, n_col, group):
            for s in range(first, first + group):
                strip_copy(s).wait()
            for s in range(first, first + group):
                tsend[s] = project(strips[s])

    x_copy.wait()
    pl.semaphore_wait(barrier, expected)

    @pl.when(is_holder)
    def _():
        for s in range(n_col - 1):
            table_send_copy(s).start()
        table[...] = tsend[n_col - 1]

    @pl.when(has_left)
    def _():
        for copy in to_left:
            copy.start()

    @pl.when(has_right)
    def _():
        for copy in to_right:
            copy.start()

    @pl.when(gives_corner)
    def _():
        corner_copy.wait()
        csend[...] = project(corner_x[...])

    @pl.when(corner_away)
    def _():
        corner_send_copy().start()

    @pl.when(gives_corner & takes_corner)
    def _():
        corner[...] = csend[...]

    used = 2 * heads * half_t
    wq_copy.wait()
    wg_copy.wait()
    wkv_copy.wait()
    shift_copy.wait()
    x_own = xs[pl.ds(0, atoms)]
    queries = dot(x_own, wq[...])
    gates = jax.nn.sigmoid(dot(x_own, wg[...]))
    lanes = lax.broadcasted_iota(jnp.int32, (atoms, width), 1)
    local_tok = tokens - tok_dev * me
    upper = local_tok >= half_t
    place = jnp.where(upper, (local_tok - half_t) * 8 + heads, local_tok * 8)
    place = jnp.transpose(jnp.broadcast_to(place, (width, 2 * width)))[:atoms]
    mark = used + lax.broadcasted_iota(jnp.int32, (atoms, width), 0) // QB
    for h in range(heads):
        q_h = jnp.where(lanes // head_dim == h, queries, 0.0).astype(BF16)
        hot_h = ((lanes == place + h) | (lanes == mark)).astype(F32).astype(BF16)
        low, high = pl.ds(h * tail, tail), pl.ds(heads * tail + h * margin, margin)
        lhs[low, pl.ds(0, width)] = q_h[:tail]
        lhs[low, pl.ds(width, width)] = hot_h[:tail]
        lhs[high, pl.ds(0, width)] = q_h[tail:]
        lhs[high, pl.ds(width, width)] = hot_h[tail:]
    member = lax.broadcasted_iota(jnp.int32, (32, atoms), 0) == (codes - tok_dev * me)[:, :atoms]
    member = member.astype(F32)
    count = jnp.sum(member, axis=1, keepdims=True)
    inverse = 1.0 / jnp.maximum(count, 1.0)
    member = member.astype(BF16)

    head_of = lax.broadcasted_iota(jnp.int32, (width, width), 1) // head_dim

    def place_keyval(b, keyval):
        rhs[b, pl.ds(0, width), :] = jnp.transpose(keyval[:, :width]).astype(BF16)
        for h in range(heads):
            vals[b, h, :, pl.ds(0, width)] = jnp.where(
                head_of == h, keyval[:, width:], 0.0
            ).astype(BF16)

    for h in range(heads):
        mine = (head_of == h).astype(F32).astype(BF16)
        for b in range(3):
            vals[b, h, :, pl.ds(width, width)] = mine

    place_keyval(0, dot(xs[pl.ds(0, width)], wkv[...]))
    side = lax.broadcasted_iota(jnp.int32, (1, width), 1)
    rest_rows = width - used
    sub = lax.broadcasted_iota(jnp.int32, (rest_rows, width), 0)
    starts = jnp.zeros((rest_rows, width), jnp.int32)
    n_blocks = atoms // QB
    for b in range(n_blocks):
        starts = jnp.where(sub == b, QB * b - KW // 2 + QB // 2 + shift[b], starts)

    def place_mask(b, at, code):
        inside = (at >= starts) & (at < starts + KW)
        value = jnp.where(inside, jnp.where(code >= 0, 0.0, DEAD), OUTSIDE)
        rhs[b, pl.ds(width + used, rest_rows), :] = jnp.where(sub < n_blocks, value, 0.0).astype(
            BF16
        )
        for k in (2, 3):
            rhs[b, pl.ds(k * width + used, rest_rows), :] = jnp.zeros((rest_rows, width), BF16)

    place_mask(0, side, codes0)
    tail_copy.wait()

    @pl.when(has_left)
    def _():
        for copy in to_right:
            copy.wait_recv()

    @pl.when(has_right)
    def _():
        for copy in to_left:
            copy.wait_recv()

    keyval = dot(xs[pl.ds(width, 2 * width)], wkv[...])
    place_keyval(1, keyval[:width])
    place_keyval(2, keyval[width:])
    codes_a = jnp.where(side < margin, codes1, codes_s[1][0:1])
    codes_b = jnp.where(side < margin, codes1, codes_s[2][0:1])
    place_mask(1, jnp.where(side < margin, side + width, side - width), codes_a)
    place_mask(2, side + width, codes_b)

    @pl.when(jnp.logical_not(is_holder))
    def _():
        table_send_copy(0).wait_recv()

    @pl.when(corner_comes)
    def _():
        corner_send_copy().wait_recv()

    main = table[...] * math.sqrt(head_dim)
    edge = corner[...] * math.sqrt(head_dim)
    stacked = jnp.concatenate(
        [
            jnp.concatenate(
                [main[:, WIDE * t : WIDE * (t + 1)], edge[:, SIDE * t : SIDE * (t + 1)]], axis=1
            )
            for t in range(half_t)
        ],
        axis=0,
    )
    first_token = hold_col * tok_cols + strip_start(col)

    def place_bias(b, code):
        index = jnp.broadcast_to((code - first_token) & (width - 1), (used, width))
        whole = jnp.take_along_axis(stacked, index, axis=1, mode="promise_in_bounds")
        high = whole.astype(BF16)
        rest = whole - high.astype(F32)
        mid = rest.astype(BF16)
        rhs[b, pl.ds(width, used), :] = high
        rhs[b, pl.ds(2 * width, used), :] = mid
        rhs[b, pl.ds(3 * width, used), :] = (rest - mid.astype(F32)).astype(BF16)

    place_bias(0, codes0)
    place_bias(1, codes_a)
    place_bias(2, codes_b)
    log_scale = math.log2(math.e) / math.sqrt(head_dim)

    def attend(first_row, n_rows, which):
        both = lhs[pl.ds(first_row, heads * n_rows), :]
        hot = both[:, width:]
        left = jnp.concatenate([both, hot, hot], axis=1)
        scores = dot(left, jnp.concatenate([rhs[0], rhs[which]], axis=1))
        parts = []
        for h in range(heads):
            part = scores[h * n_rows : (h + 1) * n_rows]
            top = jnp.max(part, axis=1, keepdims=True)
            parts.append(jnp.exp2((part - top) * log_scale).astype(BF16))
        by_head = [vals[b, h] for h in range(heads) for b in (0, which)]
        mixed = dot(jnp.concatenate(parts, axis=1), jnp.concatenate(by_head, axis=0))
        return mixed[:, :width] / mixed[:, width:]

    out_a = attend(0, tail, 1)
    out_b = attend(heads * tail, margin, 2)
    attended = (gates * jnp.concatenate([out_a, out_b], axis=0)).astype(BF16)
    wo_copy.wait()
    new_atoms = (x_own.astype(F32) + dot(attended, wo[...])).astype(BF16)
    atoms_out[...] = new_atoms
    wa_copy.wait()
    share = wa_in.shape[1] // n_col
    lifted = jnp.maximum(dot(new_atoms, wa[...]), 0.0).astype(BF16)
    means = (dot(member, lifted) * inverse)[:tok_dev]
    for c in range(n_col):
        if c * share + width <= means.shape[1]:
            piece = means[:, c * share : c * share + width]
        else:
            piece = pltpu.roll(means[:, -width:], share, 1)
        tok_send[c] = piece.astype(BF16)

    def tok_copy(other):
        return pltpu.make_async_remote_copy(
            src_ref=tok_send.at[other],
            dst_ref=tok_recv.at[col],
            send_sem=tok_ssem,
            recv_sem=tok_rsem,
            device_id=(row, other),
            device_id_type=MESH,
        )

    for step in range(1, n_col):
        tok_copy((col + step) % n_col).start()
    tok_recv[col] = tok_send[col]
    others = pl.ds(0, n_col - 1)
    all_tokens = pltpu.make_async_remote_copy(
        src_ref=tok_send.at[others],
        dst_ref=tok_recv.at[others],
        send_sem=tok_ssem,
        recv_sem=tok_rsem,
        device_id=(row, (col + 1) % n_col),
        device_id_type=MESH,
    )
    all_tokens.wait_recv()

    all_tokens.wait_send()

    @pl.when(is_holder)
    def _():
        pltpu.make_async_remote_copy(
            src_ref=tsend.at[others],
            dst_ref=tsend.at[others],
            send_sem=table_send,
            recv_sem=table_recv,
            device_id=(row, (col + 1) % n_col),
            device_id_type=MESH,
        ).wait_send()

    @pl.when(corner_away)
    def _():
        corner_send_copy().wait_send()

    @pl.when(has_left)
    def _():
        for copy in to_left:
            copy.wait_send()

    @pl.when(has_right)
    def _():
        for copy in to_right:
            copy.wait_send()


def finish(atoms_ref, gathered, atoms_out, token_out, token_v, sems):
    atoms_copy = pltpu.make_async_copy(atoms_ref, atoms_out, sems.at[0])
    atoms_copy.start()
    rows = jnp.concatenate(
        [gathered[c].astype(F32) for c in range(gathered.shape[0])], axis=0
    )
    token_v[...] = rows.astype(BF16)[:, : token_v.shape[1]]
    token_copy = pltpu.make_async_copy(token_v, token_out, sems.at[1])
    token_copy.start()
    atoms_copy.wait()
    token_copy.wait()


def per_device(n_row, n_col, *args):
    x, pair, w_pair, w_query, w_keyval, w_gate, w_out, w_agg, tok, shift, mask = args
    w_pair = w_pair.T
    atoms, width = x.shape
    tok_rows, tok_cols, chan = pair.shape
    heads = w_pair.shape[0]
    tok_dev = tok_rows // n_col
    half_t = tok_dev // 2
    ct = w_agg.shape[1]
    margin = KW // 2
    hbm = pl.BlockSpec(memory_space=pltpu.HBM)
    vmem = pl.BlockSpec(memory_space=pltpu.VMEM)
    dma = pltpu.SemaphoreType.DMA
    scratch = [
        pltpu.VMEM((3 * width, width), BF16),
        pltpu.VMEM((n_col, tok_dev, WIDE, chan), BF16),
        pltpu.VMEM((tok_dev, SIDE, chan), BF16),
        pltpu.VMEM(w_pair.shape, BF16),
        pltpu.VMEM(w_query.shape, BF16),
        pltpu.VMEM(w_keyval.shape, BF16),
        pltpu.VMEM(w_gate.shape, BF16),
        pltpu.VMEM(w_out.shape, BF16),
        pltpu.VMEM(w_agg.shape, BF16),
        pltpu.VMEM(tok.shape, jnp.int32),
        pltpu.VMEM(mask.shape, jnp.int32),
        pltpu.SMEM(shift.shape, jnp.int32),
        pltpu.VMEM((n_col, 2 * heads, half_t * WIDE), F32),
        pltpu.VMEM((2 * heads, half_t * SIDE), F32),
        pltpu.VMEM((2 * heads, half_t * WIDE), F32),
        pltpu.VMEM((2 * heads, half_t * SIDE), F32),
        pltpu.VMEM((2, 8, width), jnp.int32),
        pltpu.VMEM((3, 8, width), jnp.int32),
        pltpu.VMEM((heads * atoms, 2 * width), BF16),
        pltpu.VMEM((3, 4 * width, width), BF16),
        pltpu.VMEM((3, heads, width, 2 * width), BF16),
        pltpu.VMEM((n_col, tok_dev, width), BF16),
        dma((12,)),
        dma((n_col,)),
        dma((4,)),
        dma((4,)),
        dma,
        dma,
        dma,
        dma,
        dma,
        dma,
    ]
    inputs = (x, pair, w_pair, w_query, w_keyval, w_gate, w_out, w_agg, tok, shift, mask)
    inputs = [pltpu.with_memory_space_constraint(a, pltpu.HBM) for a in inputs]
    new_atoms, gathered = pl.pallas_call(
        functools.partial(kernel, n_row, n_col),
        out_shape=(
            pltpu.VMEM((atoms, width), BF16),
            pltpu.VMEM((n_col, tok_dev, width), BF16),
        ),
        in_specs=[hbm] * 11,
        out_specs=(vmem, vmem),
        scratch_shapes=scratch,
        compiler_params=pltpu.CompilerParams(
            collective_id=0, has_side_effects=True, vmem_limit_bytes=40 * 1024 * 1024
        ),
        name="atom_block",
    )(*inputs)
    return pl.pallas_call(
        finish,
        out_shape=(
            pltpu.HBM((atoms, width), BF16),
            pltpu.HBM((tok_rows, ct // n_col), BF16),
        ),
        in_specs=[vmem, vmem],
        out_specs=(hbm, hbm),
        scratch_shapes=[pltpu.VMEM((tok_rows, ct // n_col), BF16), dma((2,))],
        compiler_params=pltpu.CompilerParams(vmem_limit_bytes=8 * 1024 * 1024),
        name="write_out",
    )(new_atoms, gathered)


def solution(mesh):
    n_row, n_col = mesh.shape["row"], mesh.shape["col"]
    split = P(("row", "col"))
    in_specs = (
        P(("row", "col"), None),
        P("row", "col", None),
        P(),
        P(),
        P(),
        P(),
        P(),
        P(),
        split,
        split,
        split,
    )
    out_specs = (P(("row", "col"), None), P("row", "col"))
    return jax.shard_map(
        functools.partial(per_device, n_row, n_col),
        mesh=mesh,
        in_specs=in_specs,
        out_specs=out_specs,
        check_vma=False,
    )
```

```python
import functools
import math

import jax
import jax.numpy as jnp
from jax import lax
from jax.experimental import pallas as pl
from jax.experimental.pallas import tpu as pltpu
from jax.sharding import PartitionSpec as P

MESH = pl.DeviceIdType.MESH

QB = 32
KW = 128
WIDE = 72
OUTSIDE = -(2.0**126)
DEAD = -(2.0**100)
F32 = jnp.float32
BF16 = jnp.bfloat16


def dot(a, b):
    return jnp.dot(a, b, preferred_element_type=F32)


def dot_nt(a, b):
    return lax.dot_general(a, b, (((1,), (1,)), ((), ())), preferred_element_type=F32)


def kernel(
    n_row,
    n_col,
    x_in,
    pair_in,
    wp_in,
    wq_in,
    wkv_in,
    wg_in,
    wo_in,
    wa_in,
    tok_in,
    shift_in,
    mask_in,
    atoms_out,
    tok_recv,
    xs,
    strips,
    corner_x,
    wp,
    wq,
    wkv,
    wg,
    wo,
    wa,
    wa_pad,
    tok,
    mask,
    shift,
    tsend,
    csend,
    table,
    corner,
    messages,
    codes_s,
    lhs,
    rhs,
    vals,
    tok_send,
    in_sem,
    strip_sem,
    corner_sem,
    halo_send,
    halo_recv,
    table_send,
    table_recv,
    corner_send,
    corner_recv,
    tok_ssem,
    tok_rsem,
):
    row = lax.axis_index("row")
    col = lax.axis_index("col")
    me = row * n_col + col
    n_dev = n_row * n_col
    atoms, width = x_in.shape
    tok_rows, tok_cols, chan = pair_in.shape
    tok_dev = tok_rows // n_col
    half_t = tok_dev // 2
    heads = wp_in.shape[0]
    head_dim = width // heads
    margin = KW // 2
    per_col = tok_cols // tok_rows
    hold_col = row // per_col
    odd = row % per_col == per_col - 1
    even = row % per_col == 0
    is_holder = col == hold_col
    base = (row % per_col) * tok_rows
    has_left = me > 0
    has_right = me < n_dev - 1

    def nth(s):
        half = n_col // 2
        turn = (half // 2, 1, half - 1, 0)[s % half]
        side = col // half if s >= half else 1 - col // half
        return side * half + (col + turn) % half

    def strip_start(j):
        want = jnp.maximum(base + tok_dev * (j - 1), 0)
        return jnp.minimum(want, tok_cols - WIDE)

    barrier = pltpu.get_barrier_semaphore()

    for step in range(1, n_col):
        other = (col + step) % n_col
        pl.semaphore_signal(barrier, inc=1, device_id=(row, other), device_id_type=MESH)

    up_row = (col == 0) & has_left
    down_row = (col == n_col - 1) & has_right
    left_id = (jnp.where(col > 0, row, row - 1), (col + n_col - 1) % n_col)
    right_id = (jnp.where(col < n_col - 1, row, row + 1), (col + 1) % n_col)

    @pl.when(up_row)
    def _():
        pl.semaphore_signal(barrier, inc=1, device_id=left_id, device_id_type=MESH)

    @pl.when(down_row)
    def _():
        pl.semaphore_signal(barrier, inc=1, device_id=right_id, device_id_type=MESH)

    expected = n_col - 1 + up_row.astype(jnp.int32) + down_row.astype(jnp.int32)

    def local(i, src, dst):
        return pltpu.make_async_copy(src, dst, in_sem.at[i])

    tail = atoms - margin
    x_copy = local(0, x_in, xs.at[pl.ds(0, atoms)])
    tail_copy = local(1, x_in.at[pl.ds(tail, margin)], xs.at[pl.ds(2 * width, margin)])
    toks_copy = local(2, tok_in, tok)
    mask_copy = local(3, mask_in, mask)
    wp_copy = local(4, wp_in, wp)
    wq_copy = local(5, wq_in, wq)
    wg_copy = local(6, wg_in, wg)
    wkv_copy = local(7, wkv_in, wkv)
    shift_copy = local(8, shift_in, shift)
    wo_copy = local(9, wo_in, wo)
    wa_copy = local(10, wa_in, wa)

    def window_copies(first_row, first_col, dst, sems):
        return [
            pltpu.make_async_copy(
                pair_in.at[pl.ds(first_row + p * half_t, half_t), pl.ds(first_col, WIDE)],
                dst.at[:, pl.ds(p * WIDE, WIDE)],
                sems.at[p],
            )
            for p in range(2)
        ]

    def strip_copies(s):
        j = nth(s)
        start = pl.multiple_of(strip_start(j), 8)
        return window_copies(tok_dev * j, start, strips.at[s], strip_sem.at[s])

    x_copy.start()
    toks_copy.start()
    mask_copy.start()
    wp_copy.start()

    @pl.when(is_holder)
    def _():
        for s in range(n_col):
            for copy in strip_copies(s):
                copy.start()

    wq_copy.start()
    wg_copy.start()
    tail_copy.start()
    wkv_copy.start()
    shift_copy.start()
    wo_copy.start()
    wa_copy.start()

    corner_to = jnp.where(even, 0, n_col - 1)
    gives_corner = (even & (col == hold_col - 1)) | (odd & (col == hold_col + 1))
    takes_corner = (up_row & even) | (down_row & odd)
    corner_comes = takes_corner & jnp.logical_not(gives_corner)
    corner_away = gives_corner & jnp.logical_not(takes_corner)
    corner_col = pl.multiple_of(jnp.where(even, tok_cols - WIDE, 0), 8)
    corner_row = pl.multiple_of(jnp.where(even, 0, tok_rows - tok_dev), 8)
    corner_copies = window_copies(corner_row, corner_col, corner_x, corner_sem)

    @pl.when(gives_corner)
    def _():
        for copy in corner_copies:
            copy.start()

    @pl.when(jnp.logical_not(corner_comes))
    def _():
        corner[...] = jnp.zeros_like(corner)

    def project(block):
        w_one = wp[...].astype(F32)
        w_rows = jnp.concatenate([w_one, w_one], axis=0)
        first_half = lax.broadcasted_iota(jnp.int32, w_rows.shape, 0) < heads
        w_both = jnp.concatenate(
            [jnp.where(first_half, w_rows, 0.0), jnp.where(first_half, 0.0, w_rows)], axis=1
        ).astype(BF16)
        flat = block.reshape(tok_dev * WIDE, chan)
        low, high = flat[: half_t * WIDE], flat[half_t * WIDE :]
        out = dot_nt(w_both, jnp.concatenate([low, high], axis=1))
        spare = table.shape[1] - out.shape[1]
        return jnp.concatenate([out, jnp.zeros((2 * heads, spare), F32)], axis=1)

    def corner_send_copy():
        return pltpu.make_async_remote_copy(
            src_ref=csend,
            dst_ref=corner,
            send_sem=corner_send,
            recv_sem=corner_recv,
            device_id=(row, corner_to),
            device_id_type=MESH,
        )

    def table_send_copy(s):
        j = nth(s)
        return pltpu.make_async_remote_copy(
            src_ref=tsend.at[s],
            dst_ref=table,
            send_sem=table_send,
            recv_sem=table_recv,
            device_id=(row, j),
            device_id_type=MESH,
        )

    toks_copy.wait()
    mask_copy.wait()
    spare = 2 * width - atoms
    tokens = jnp.concatenate(
        [tok[...].reshape(1, atoms), jnp.full((1, spare), -1, jnp.int32)], axis=1
    )
    masks = jnp.concatenate(
        [mask[...].reshape(1, atoms), jnp.zeros((1, spare), jnp.int32)], axis=1
    )
    codes = jnp.where(masks == 1, tokens, -1)
    codes0, codes1 = codes[:, :width], codes[:, width:]
    messages[0] = jnp.broadcast_to(pltpu.roll(codes0, margin, 1), (8, width))
    messages[1] = jnp.broadcast_to(pltpu.roll(codes1, margin, 1), (8, width))

    def halo(i, src, dst, device):
        return pltpu.make_async_remote_copy(
            src_ref=src,
            dst_ref=dst,
            send_sem=halo_send.at[i],
            recv_sem=halo_recv.at[i],
            device_id=device,
            device_id_type=MESH,
        )

    x_left, x_right = pl.ds(atoms, margin), pl.ds(2 * width + margin, margin)
    to_left = (
        halo(0, xs.at[pl.ds(0, margin)], xs.at[x_right], left_id),
        halo(1, messages.at[0], codes_s.at[2], left_id),
    )
    to_right = (
        halo(2, xs.at[pl.ds(tail, margin)], xs.at[x_left], right_id),
        halo(3, messages.at[1], codes_s.at[1], right_id),
    )

    @pl.when(jnp.logical_not(has_left))
    def _():
        xs[x_left] = jnp.zeros((margin, width), BF16)
        codes_s[1] = jnp.full((8, width), -1, jnp.int32)

    @pl.when(jnp.logical_not(has_right))
    def _():
        xs[x_right] = jnp.zeros((margin, width), BF16)
        codes_s[2] = jnp.full((8, width), -1, jnp.int32)

    x_copy.wait()

    def send_halos():
        @pl.when(has_left)
        def _():
            for copy in to_left:
                copy.start()

        @pl.when(has_right)
        def _():
            for copy in to_right:
                copy.start()

    @pl.when(jnp.logical_not(is_holder))
    def _():
        pl.semaphore_wait(barrier, expected)
        send_halos()

    @pl.when(gives_corner)
    def _():
        wp_copy.wait()
        for copy in corner_copies:
            copy.wait()
        csend[...] = project(corner_x[...])

    @pl.when(corner_away)
    def _():
        corner_send_copy().start()

    @pl.when(gives_corner & takes_corner)
    def _():
        corner[...] = csend[...]

    used = 2 * heads * half_t
    wq_copy.wait()
    wg_copy.wait()
    wkv_copy.wait()
    shift_copy.wait()
    x_own = xs[pl.ds(0, atoms)]
    queries = dot(x_own, wq[...])
    gates = jax.nn.sigmoid(dot(x_own, wg[...]))
    lanes = lax.broadcasted_iota(jnp.int32, (atoms, width), 1)
    local_tok = tokens - tok_dev * me
    second = (local_tok >= half_t).astype(jnp.int32)
    within = local_tok - half_t * second
    lower = (within >= half_t // 2).astype(jnp.int32)
    place = 2 * heads * (2 * within - half_t * lower + second) + heads * lower
    place = jnp.transpose(jnp.broadcast_to(place, (width, 2 * width)))[:atoms]
    mark = used + lax.broadcasted_iota(jnp.int32, (atoms, width), 0) // QB
    for h in range(heads):
        q_h = jnp.where(lanes // head_dim == h, queries, 0.0).astype(BF16)
        hot_h = ((lanes == place + h) | (lanes == mark)).astype(F32).astype(BF16)
        low, high = pl.ds(h * tail, tail), pl.ds(heads * tail + h * margin, margin)
        lhs[low, pl.ds(0, width)] = q_h[:tail]
        lhs[low, pl.ds(width, width)] = hot_h[:tail]
        lhs[high, pl.ds(0, width)] = q_h[tail:]
        lhs[high, pl.ds(width, width)] = hot_h[tail:]
    wa_copy.wait()
    share = wa_in.shape[1] // n_col
    for c in range(n_col):
        wa_pad[:, c * width : (c + 1) * width] = jnp.concatenate(
            [wa[:, c * share : (c + 1) * share], jnp.zeros((width, width - share), BF16)], axis=1
        )
    member = lax.broadcasted_iota(jnp.int32, (32, atoms), 0) == (codes - tok_dev * me)[:, :atoms]
    member = member.astype(F32)
    count = jnp.sum(member, axis=1, keepdims=True)
    inverse = 1.0 / jnp.maximum(count, 1.0)
    member = member.astype(BF16)

    @pl.when(is_holder)
    def _():
        wp_copy.wait()
        group = n_col // 2
        for begin in range(0, n_col, group):
            for s in range(begin, begin + group):
                for copy in strip_copies(s):
                    copy.wait()
            for s in range(begin, begin + group):
                tsend[s] = project(strips[s])
            if begin == 0:
                pl.semaphore_wait(barrier, expected)
                send_halos()
            for s in range(begin, min(begin + group, n_col - 1)):
                table_send_copy(s).start()
        table[...] = tsend[n_col - 1]

    @pl.when(jnp.logical_not(is_holder | gives_corner))
    def _():
        wp_copy.wait()

    head_of = lax.broadcasted_iota(jnp.int32, (width, width), 1) // head_dim

    def place_keyval(b, keyval):
        rhs[b, pl.ds(0, width), :] = jnp.transpose(keyval[:, :width]).astype(BF16)
        for h in range(heads):
            vals[b, h, :, pl.ds(0, width)] = jnp.where(
                head_of == h, keyval[:, width:], 0.0
            ).astype(BF16)

    for h in range(heads):
        mine = (head_of == h).astype(F32).astype(BF16)
        for b in range(3):
            vals[b, h, :, pl.ds(width, width)] = mine

    place_keyval(0, dot(xs[pl.ds(0, width)], wkv[...]))
    side = lax.broadcasted_iota(jnp.int32, (1, width), 1)
    rest_rows = width - used
    sub = lax.broadcasted_iota(jnp.int32, (rest_rows, width), 0)
    starts = jnp.zeros((rest_rows, width), jnp.int32)
    n_blocks = atoms // QB
    for b in range(n_blocks):
        starts = jnp.where(sub == b, QB * b - KW // 2 + QB // 2 + shift[b], starts)

    def place_mask(b, at, code):
        inside = (at >= starts) & (at < starts + KW)
        value = jnp.where(inside, jnp.where(code >= 0, 0.0, DEAD), OUTSIDE)
        rhs[b, pl.ds(width + used, rest_rows), :] = jnp.where(sub < n_blocks, value, 0.0).astype(
            BF16
        )
        for k in (2, 3):
            rhs[b, pl.ds(k * width + used, rest_rows), :] = jnp.zeros((rest_rows, width), BF16)

    place_mask(0, side, codes0)
    tail_copy.wait()

    @pl.when(has_left)
    def _():
        for copy in to_right:
            copy.wait_recv()

    @pl.when(has_right)
    def _():
        for copy in to_left:
            copy.wait_recv()

    keyval = dot(xs[pl.ds(width, 2 * width)], wkv[...])
    place_keyval(1, keyval[:width])
    place_keyval(2, keyval[width:])
    codes_a = jnp.where(side < margin, codes1, codes_s[1][0:1])
    codes_b = jnp.where(side < margin, codes1, codes_s[2][0:1])
    place_mask(1, jnp.where(side < margin, side + width, side - width), codes_a)
    place_mask(2, side + width, codes_b)

    first_token = hold_col * tok_cols + strip_start(col)
    in_strip = lax.broadcasted_iota(jnp.int32, table.shape, 1) % WIDE
    from_low = in_strip >= jnp.where(takes_corner & even, WIDE - tok_dev, WIDE)
    from_high = in_strip < jnp.where(takes_corner & odd, tok_dev, 0)
    from_corner = from_low | from_high

    @pl.when(jnp.logical_not(is_holder))
    def _():
        table_send_copy(0).wait_recv()

    @pl.when(corner_comes)
    def _():
        corner_send_copy().wait_recv()

    main = jnp.where(from_corner, corner[...], table[...]) * math.sqrt(head_dim)

    def place_bias(b, code):
        index = code - first_token
        index = jnp.where(index < 0, index + WIDE, jnp.where(index >= WIDE, index - WIDE, index))
        index = jnp.broadcast_to(jnp.clip(index, 0, WIDE - 1), (2 * heads, width))
        rows = []
        for t in range(half_t):
            a, at = divmod(WIDE * t, width)
            flat = index + at

            def take(k):
                tile = main[:, k * width : (k + 1) * width]
                return jnp.take_along_axis(
                    tile, flat & (width - 1), axis=1, mode="promise_in_bounds"
                )

            one = take(a)
            rows.append(one if at + WIDE <= width else jnp.where(flat < width, one, take(a + 1)))
        whole = jnp.concatenate(rows, axis=0)
        high = whole.astype(BF16)
        rest = whole - high.astype(F32)
        mid = rest.astype(BF16)
        rhs[b, pl.ds(width, used), :] = high
        rhs[b, pl.ds(2 * width, used), :] = mid
        rhs[b, pl.ds(3 * width, used), :] = (rest - mid.astype(F32)).astype(BF16)

    place_bias(0, codes0)
    place_bias(1, codes_a)
    place_bias(2, codes_b)
    log_scale = math.log2(math.e) / math.sqrt(head_dim)

    def attend(first_row, n_rows, which):
        both = lhs[pl.ds(first_row, heads * n_rows), :]
        hot = both[:, width:]
        left = jnp.concatenate([both, hot, hot], axis=1)
        scores = dot(left, jnp.concatenate([rhs[0], rhs[which]], axis=1))
        parts = []
        for h in range(heads):
            part = scores[h * n_rows : (h + 1) * n_rows]
            top = jnp.max(part, axis=1, keepdims=True)
            parts.append(jnp.exp2((part - top) * log_scale).astype(BF16))
        by_head = [vals[b, h] for h in range(heads) for b in (0, which)]
        mixed = dot(jnp.concatenate(parts, axis=1), jnp.concatenate(by_head, axis=0))
        return mixed[:, :width] / mixed[:, width:]

    out_a = attend(0, tail, 1)
    out_b = attend(heads * tail, margin, 2)
    attended = (gates * jnp.concatenate([out_a, out_b], axis=0)).astype(BF16)
    wo_copy.wait()
    new_atoms = (x_own.astype(F32) + dot(attended, wo[...])).astype(BF16)
    atoms_out[...] = new_atoms
    lifted = jnp.maximum(dot(new_atoms, wa_pad[...]), 0.0).astype(BF16)
    means = (dot(member, lifted) * inverse)[:tok_dev].astype(BF16)
    for c in range(n_col):
        tok_send[c] = means[:, c * width : (c + 1) * width]

    def tok_copy(other):
        return pltpu.make_async_remote_copy(
            src_ref=tok_send.at[other],
            dst_ref=tok_recv.at[col],
            send_sem=tok_ssem,
            recv_sem=tok_rsem,
            device_id=(row, other),
            device_id_type=MESH,
        )

    for s in range(n_col - 1):
        tok_copy(nth(s)).start()
    tok_recv[col] = tok_send[col]
    others = pl.ds(0, n_col - 1)
    all_tokens = pltpu.make_async_remote_copy(
        src_ref=tok_send.at[others],
        dst_ref=tok_recv.at[others],
        send_sem=tok_ssem,
        recv_sem=tok_rsem,
        device_id=(row, (col + 1) % n_col),
        device_id_type=MESH,
    )
    all_tokens.wait_recv()

    all_tokens.wait_send()

    @pl.when(is_holder)
    def _():
        pltpu.make_async_remote_copy(
            src_ref=tsend.at[others],
            dst_ref=tsend.at[others],
            send_sem=table_send,
            recv_sem=table_recv,
            device_id=(row, (col + 1) % n_col),
            device_id_type=MESH,
        ).wait_send()

    @pl.when(corner_away)
    def _():
        corner_send_copy().wait_send()

    @pl.when(has_left)
    def _():
        for copy in to_left:
            copy.wait_send()

    @pl.when(has_right)
    def _():
        for copy in to_right:
            copy.wait_send()


def finish(atoms_ref, gathered, atoms_out, token_out, token_v, sems):
    atoms_copy = pltpu.make_async_copy(atoms_ref, atoms_out, sems.at[0])
    atoms_copy.start()
    rows = jnp.concatenate(
        [gathered[c].astype(F32) for c in range(gathered.shape[0])], axis=0
    )
    token_v[...] = rows.astype(BF16)[:, : token_v.shape[1]]
    token_copy = pltpu.make_async_copy(token_v, token_out, sems.at[1])
    token_copy.start()
    atoms_copy.wait()
    token_copy.wait()


def per_device(n_row, n_col, *args):
    x, pair, w_pair, w_query, w_keyval, w_gate, w_out, w_agg, tok, shift, mask = args
    w_pair = w_pair.T
    atoms, width = x.shape
    tok_rows, tok_cols, chan = pair.shape
    heads = w_pair.shape[0]
    tok_dev = tok_rows // n_col
    half_t = tok_dev // 2
    ct = w_agg.shape[1]
    margin = KW // 2
    lanes = -(-half_t * WIDE // 128) * 128
    hbm = pl.BlockSpec(memory_space=pltpu.HBM)
    vmem = pl.BlockSpec(memory_space=pltpu.VMEM)
    dma = pltpu.SemaphoreType.DMA
    scratch = [
        pltpu.VMEM((3 * width, width), BF16),
        pltpu.VMEM((n_col, half_t, 2 * WIDE, chan), BF16),
        pltpu.VMEM((half_t, 2 * WIDE, chan), BF16),
        pltpu.VMEM(w_pair.shape, BF16),
        pltpu.VMEM(w_query.shape, BF16),
        pltpu.VMEM(w_keyval.shape, BF16),
        pltpu.VMEM(w_gate.shape, BF16),
        pltpu.VMEM(w_out.shape, BF16),
        pltpu.VMEM(w_agg.shape, BF16),
        pltpu.VMEM((width, n_col * width), BF16),
        pltpu.VMEM(tok.shape, jnp.int32),
        pltpu.VMEM(mask.shape, jnp.int32),
        pltpu.SMEM(shift.shape, jnp.int32),
        pltpu.VMEM((n_col, 2 * heads, lanes), F32),
        pltpu.VMEM((2 * heads, lanes), F32),
        pltpu.VMEM((2 * heads, lanes), F32),
        pltpu.VMEM((2 * heads, lanes), F32),
        pltpu.VMEM((2, 8, width), jnp.int32),
        pltpu.VMEM((3, 8, width), jnp.int32),
        pltpu.VMEM((heads * atoms, 2 * width), BF16),
        pltpu.VMEM((3, 4 * width, width), BF16),
        pltpu.VMEM((3, heads, width, 2 * width), BF16),
        pltpu.VMEM((n_col, tok_dev, width), BF16),
        dma((11,)),
        dma((n_col, 2)),
        dma((2,)),
        dma((4,)),
        dma((4,)),
        dma,
        dma,
        dma,
        dma,
        dma,
        dma,
    ]
    inputs = (x, pair, w_pair, w_query, w_keyval, w_gate, w_out, w_agg, tok, shift, mask)
    inputs = [pltpu.with_memory_space_constraint(a, pltpu.HBM) for a in inputs]
    new_atoms, gathered = pl.pallas_call(
        functools.partial(kernel, n_row, n_col),
        out_shape=(
            pltpu.VMEM((atoms, width), BF16),
            pltpu.VMEM((n_col, tok_dev, width), BF16),
        ),
        in_specs=[hbm] * 11,
        out_specs=(vmem, vmem),
        scratch_shapes=scratch,
        compiler_params=pltpu.CompilerParams(
            collective_id=0, has_side_effects=True, vmem_limit_bytes=40 * 1024 * 1024
        ),
        name="atom_block",
    )(*inputs)
    return pl.pallas_call(
        finish,
        out_shape=(
            pltpu.HBM((atoms, width), BF16),
            pltpu.HBM((tok_rows, ct // n_col), BF16),
        ),
        in_specs=[vmem, vmem],
        out_specs=(hbm, hbm),
        scratch_shapes=[pltpu.VMEM((tok_rows, ct // n_col), BF16), dma((2,))],
        compiler_params=pltpu.CompilerParams(vmem_limit_bytes=8 * 1024 * 1024),
        name="write_out",
    )(new_atoms, gathered)


def solution(mesh):
    n_row, n_col = mesh.shape["row"], mesh.shape["col"]
    split = P(("row", "col"))
    in_specs = (
        P(("row", "col"), None),
        P("row", "col", None),
        P(),
        P(),
        P(),
        P(),
        P(),
        P(),
        split,
        split,
        split,
    )
    out_specs = (P(("row", "col"), None), P("row", "col"))
    return jax.shard_map(
        functools.partial(per_device, n_row, n_col),
        mesh=mesh,
        in_specs=in_specs,
        out_specs=out_specs,
        check_vma=False,
    )
```

```python
import functools
import math

import jax
import jax.numpy as jnp
from jax import lax
from jax.experimental import pallas as pl
from jax.experimental.pallas import tpu as pltpu
from jax.sharding import PartitionSpec as P

MESH = pl.DeviceIdType.MESH

QB = 32
KW = 128
WIDE = 72
OUTSIDE = -(2.0**126)
DEAD = -(2.0**100)
F32 = jnp.float32
BF16 = jnp.bfloat16


def dot(a, b):
    return jnp.dot(a, b, preferred_element_type=F32)


def dot_nt(a, b):
    return lax.dot_general(a, b, (((1,), (1,)), ((), ())), preferred_element_type=F32)


def kernel(
    n_row,
    n_col,
    x_in,
    pair_in,
    wp_in,
    wq_in,
    wkv_in,
    wg_in,
    wo_in,
    wa_in,
    tok_in,
    shift_in,
    mask_in,
    atoms_out,
    tok_recv,
    xs,
    strips,
    corner_x,
    wp,
    wq,
    wkv,
    wg,
    wo,
    wa,
    wa_pad,
    tok,
    mask,
    shift,
    tsend,
    csend,
    table,
    corner,
    messages,
    codes_s,
    lhs,
    rhs,
    vals,
    tok_send,
    in_sem,
    strip_sem,
    corner_sem,
    halo_send,
    halo_recv,
    table_send,
    table_recv,
    corner_send,
    corner_recv,
    tok_ssem,
    tok_rsem,
):
    row = lax.axis_index("row")
    col = lax.axis_index("col")
    me = row * n_col + col
    n_dev = n_row * n_col
    atoms, width = x_in.shape
    tok_rows, tok_cols, chan = pair_in.shape
    tok_dev = tok_rows // n_col
    half_t = tok_dev // 2
    heads = wp_in.shape[0]
    head_dim = width // heads
    margin = KW // 2
    per_col = tok_cols // tok_rows
    hold_col = row // per_col
    odd = row % per_col == per_col - 1
    even = row % per_col == 0
    is_holder = col == hold_col
    base = (row % per_col) * tok_rows
    has_left = me > 0
    has_right = me < n_dev - 1

    def nth(s):
        half = n_col // 2
        turn = (half // 2, 1, half - 1, 0)[s % half]
        side = col // half if s >= half else 1 - col // half
        return side * half + (col + turn) % half

    def strip_start(j):
        want = jnp.maximum(base + tok_dev * (j - 1), 0)
        return jnp.minimum(want, tok_cols - WIDE)

    barrier = pltpu.get_barrier_semaphore()

    for step in range(1, n_col):
        other = (col + step) % n_col
        pl.semaphore_signal(barrier, inc=1, device_id=(row, other), device_id_type=MESH)

    up_row = (col == 0) & has_left
    down_row = (col == n_col - 1) & has_right
    left_id = (jnp.where(col > 0, row, row - 1), (col + n_col - 1) % n_col)
    right_id = (jnp.where(col < n_col - 1, row, row + 1), (col + 1) % n_col)

    @pl.when(up_row)
    def _():
        pl.semaphore_signal(barrier, inc=1, device_id=left_id, device_id_type=MESH)

    @pl.when(down_row)
    def _():
        pl.semaphore_signal(barrier, inc=1, device_id=right_id, device_id_type=MESH)

    expected = n_col - 1 + up_row.astype(jnp.int32) + down_row.astype(jnp.int32)

    def local(i, src, dst):
        return pltpu.make_async_copy(src, dst, in_sem.at[i])

    tail = atoms - margin
    x_copy = local(0, x_in, xs.at[pl.ds(0, atoms)])
    tail_copy = local(1, x_in.at[pl.ds(tail, margin)], xs.at[pl.ds(2 * width, margin)])
    toks_copy = local(2, tok_in, tok)
    mask_copy = local(3, mask_in, mask)
    wp_copy = local(4, wp_in, wp)
    wq_copy = local(5, wq_in, wq)
    wg_copy = local(6, wg_in, wg)
    wkv_copy = local(7, wkv_in, wkv)
    shift_copy = local(8, shift_in, shift)
    wo_copy = local(9, wo_in, wo)
    wa_copy = local(10, wa_in, wa)

    def window_copies(first_row, first_col, dst, sems):
        return [
            pltpu.make_async_copy(
                pair_in.at[pl.ds(first_row + p * half_t, half_t), pl.ds(first_col, WIDE)],
                dst.at[:, pl.ds(p * WIDE, WIDE)],
                sems.at[p],
            )
            for p in range(2)
        ]

    def strip_copies(s):
        j = nth(s)
        start = pl.multiple_of(strip_start(j), 8)
        return window_copies(tok_dev * j, start, strips.at[s], strip_sem.at[s])

    x_copy.start()
    toks_copy.start()
    mask_copy.start()
    wp_copy.start()

    @pl.when(is_holder)
    def _():
        for s in range(n_col):
            for copy in strip_copies(s):
                copy.start()

    wq_copy.start()
    wg_copy.start()
    tail_copy.start()
    wkv_copy.start()
    shift_copy.start()
    wo_copy.start()
    wa_copy.start()

    corner_to = jnp.where(even, 0, n_col - 1)
    gives_corner = (even & (col == hold_col - 1)) | (odd & (col == hold_col + 1))
    takes_corner = (up_row & even) | (down_row & odd)
    corner_comes = takes_corner & jnp.logical_not(gives_corner)
    corner_away = gives_corner & jnp.logical_not(takes_corner)
    corner_col = pl.multiple_of(jnp.where(even, tok_cols - WIDE, 0), 8)
    corner_row = pl.multiple_of(jnp.where(even, 0, tok_rows - tok_dev), 8)
    corner_copies = window_copies(corner_row, corner_col, corner_x, corner_sem)

    @pl.when(gives_corner)
    def _():
        for copy in corner_copies:
            copy.start()

    @pl.when(jnp.logical_not(corner_comes))
    def _():
        corner[...] = jnp.zeros_like(corner)

    def project(block):
        w_one = wp[...].astype(F32)
        w_rows = jnp.concatenate([w_one, w_one], axis=0)
        first_half = lax.broadcasted_iota(jnp.int32, w_rows.shape, 0) < heads
        w_both = jnp.concatenate(
            [jnp.where(first_half, w_rows, 0.0), jnp.where(first_half, 0.0, w_rows)], axis=1
        ).astype(BF16)
        flat = block.reshape(tok_dev * WIDE, chan)
        low, high = flat[: half_t * WIDE], flat[half_t * WIDE :]
        out = dot_nt(w_both, jnp.concatenate([low, high], axis=1))
        spare = table.shape[1] - out.shape[1]
        return jnp.concatenate([out, jnp.zeros((2 * heads, spare), F32)], axis=1)

    def corner_send_copy():
        return pltpu.make_async_remote_copy(
            src_ref=csend,
            dst_ref=corner,
            send_sem=corner_send,
            recv_sem=corner_recv,
            device_id=(row, corner_to),
            device_id_type=MESH,
        )

    def table_send_copy(s):
        j = nth(s)
        return pltpu.make_async_remote_copy(
            src_ref=tsend.at[s],
            dst_ref=table,
            send_sem=table_send,
            recv_sem=table_recv,
            device_id=(row, j),
            device_id_type=MESH,
        )

    toks_copy.wait()
    mask_copy.wait()
    spare = 2 * width - atoms
    tokens = jnp.concatenate(
        [tok[...].reshape(1, atoms), jnp.full((1, spare), -1, jnp.int32)], axis=1
    )
    masks = jnp.concatenate(
        [mask[...].reshape(1, atoms), jnp.zeros((1, spare), jnp.int32)], axis=1
    )
    codes = jnp.where(masks == 1, tokens, -1)
    codes0, codes1 = codes[:, :width], codes[:, width:]
    messages[0] = jnp.broadcast_to(pltpu.roll(codes0, margin, 1), (8, width))
    messages[1] = jnp.broadcast_to(pltpu.roll(codes1, margin, 1), (8, width))

    def halo(i, src, dst, device):
        return pltpu.make_async_remote_copy(
            src_ref=src,
            dst_ref=dst,
            send_sem=halo_send.at[i],
            recv_sem=halo_recv.at[i],
            device_id=device,
            device_id_type=MESH,
        )

    x_left, x_right = pl.ds(atoms, margin), pl.ds(2 * width + margin, margin)
    to_left = (
        halo(0, xs.at[pl.ds(0, margin)], xs.at[x_right], left_id),
        halo(1, messages.at[0], codes_s.at[2], left_id),
    )
    to_right = (
        halo(2, xs.at[pl.ds(tail, margin)], xs.at[x_left], right_id),
        halo(3, messages.at[1], codes_s.at[1], right_id),
    )

    @pl.when(jnp.logical_not(has_left))
    def _():
        xs[x_left] = jnp.zeros((margin, width), BF16)
        codes_s[1] = jnp.full((8, width), -1, jnp.int32)

    @pl.when(jnp.logical_not(has_right))
    def _():
        xs[x_right] = jnp.zeros((margin, width), BF16)
        codes_s[2] = jnp.full((8, width), -1, jnp.int32)

    x_copy.wait()

    def send_halos():
        @pl.when(has_left)
        def _():
            for copy in to_left:
                copy.start()

        @pl.when(has_right)
        def _():
            for copy in to_right:
                copy.start()

    @pl.when(jnp.logical_not(is_holder))
    def _():
        pl.semaphore_wait(barrier, expected)
        send_halos()

    @pl.when(gives_corner)
    def _():
        wp_copy.wait()
        for copy in corner_copies:
            copy.wait()
        csend[...] = project(corner_x[...])

    @pl.when(corner_away)
    def _():
        corner_send_copy().start()

    @pl.when(gives_corner & takes_corner)
    def _():
        corner[...] = csend[...]

    used = 2 * heads * half_t
    wq_copy.wait()
    wg_copy.wait()
    wkv_copy.wait()
    shift_copy.wait()
    x_own = xs[pl.ds(0, atoms)]
    queries = dot(x_own, wq[...])
    gates = jax.nn.sigmoid(dot(x_own, wg[...]))
    lanes = lax.broadcasted_iota(jnp.int32, (atoms, width), 1)
    local_tok = tokens - tok_dev * me
    second = (local_tok >= half_t).astype(jnp.int32)
    within = local_tok - half_t * second
    lower = (within >= half_t // 2).astype(jnp.int32)
    place = 2 * heads * (2 * within - half_t * lower + second) + heads * lower
    place = jnp.transpose(jnp.broadcast_to(place, (width, 2 * width)))[:atoms]
    mark = used + lax.broadcasted_iota(jnp.int32, (atoms, width), 0) // QB
    for h in range(heads):
        q_h = jnp.where(lanes // head_dim == h, queries, 0.0).astype(BF16)
        hot_h = ((lanes == place + h) | (lanes == mark)).astype(F32).astype(BF16)
        low, high = pl.ds(h * tail, tail), pl.ds(heads * tail + h * margin, margin)
        lhs[low, pl.ds(0, width)] = q_h[:tail]
        lhs[low, pl.ds(width, width)] = hot_h[:tail]
        lhs[high, pl.ds(0, width)] = q_h[tail:]
        lhs[high, pl.ds(width, width)] = hot_h[tail:]
    wa_copy.wait()
    share = wa_in.shape[1] // n_col
    for c in range(n_col):
        wa_pad[:, c * width : (c + 1) * width] = jnp.concatenate(
            [wa[:, c * share : (c + 1) * share], jnp.zeros((width, width - share), BF16)], axis=1
        )
    member = lax.broadcasted_iota(jnp.int32, (32, atoms), 0) == (codes - tok_dev * me)[:, :atoms]
    member = member.astype(F32)
    count = jnp.sum(member, axis=1, keepdims=True)
    inverse = 1.0 / jnp.maximum(count, 1.0)
    member = member.astype(BF16)

    head_of = lax.broadcasted_iota(jnp.int32, (width, width), 1) // head_dim

    def place_keyval(b, keyval):
        rhs[b, pl.ds(0, width), :] = jnp.transpose(keyval[:, :width]).astype(BF16)
        for h in range(heads):
            vals[b, h, :, pl.ds(0, width)] = jnp.where(
                head_of == h, keyval[:, width:], 0.0
            ).astype(BF16)

    for h in range(heads):
        mine = (head_of == h).astype(F32).astype(BF16)
        for b in range(3):
            vals[b, h, :, pl.ds(width, width)] = mine

    place_keyval(0, dot(xs[pl.ds(0, width)], wkv[...]))
    side = lax.broadcasted_iota(jnp.int32, (1, width), 1)
    rest_rows = width - used
    sub = lax.broadcasted_iota(jnp.int32, (rest_rows, width), 0)
    starts = jnp.zeros((rest_rows, width), jnp.int32)
    n_blocks = atoms // QB
    for b in range(n_blocks):
        starts = jnp.where(sub == b, QB * b - KW // 2 + QB // 2 + shift[b], starts)

    def place_mask(b, at, code):
        inside = (at >= starts) & (at < starts + KW)
        value = jnp.where(inside, jnp.where(code >= 0, 0.0, DEAD), OUTSIDE)
        rhs[b, pl.ds(width + used, rest_rows), :] = jnp.where(sub < n_blocks, value, 0.0).astype(
            BF16
        )
        for k in (2, 3):
            rhs[b, pl.ds(k * width + used, rest_rows), :] = jnp.zeros((rest_rows, width), BF16)

    place_mask(0, side, codes0)
    group = n_col // 2
    starts_early = hold_col % group < group // 2

    def announce():
        pl.semaphore_wait(barrier, expected)
        send_halos()
        for s in range(group):
            table_send_copy(s).start()

    @pl.when(is_holder)
    def _():
        wp_copy.wait()
        for begin in range(0, n_col, group):
            for s in range(begin, begin + group):
                for copy in strip_copies(s):
                    copy.wait()
            for s in range(begin, begin + group):
                tsend[s] = project(strips[s])
            pl.when(starts_early == (begin > 0))(announce)
        for s in range(group, n_col - 1):
            table_send_copy(s).start()
        table[...] = tsend[n_col - 1]

    @pl.when(jnp.logical_not(is_holder | gives_corner))
    def _():
        wp_copy.wait()

    tail_copy.wait()

    @pl.when(has_left)
    def _():
        for copy in to_right:
            copy.wait_recv()

    @pl.when(has_right)
    def _():
        for copy in to_left:
            copy.wait_recv()

    keyval = dot(xs[pl.ds(width, 2 * width)], wkv[...])
    place_keyval(1, keyval[:width])
    place_keyval(2, keyval[width:])
    codes_a = jnp.where(side < margin, codes1, codes_s[1][0:1])
    codes_b = jnp.where(side < margin, codes1, codes_s[2][0:1])
    place_mask(1, jnp.where(side < margin, side + width, side - width), codes_a)
    place_mask(2, side + width, codes_b)

    first_token = hold_col * tok_cols + strip_start(col)
    in_strip = lax.broadcasted_iota(jnp.int32, table.shape, 1) % WIDE
    from_low = in_strip >= jnp.where(takes_corner & even, WIDE - tok_dev, WIDE)
    from_high = in_strip < jnp.where(takes_corner & odd, tok_dev, 0)
    from_corner = from_low | from_high

    @pl.when(jnp.logical_not(is_holder))
    def _():
        table_send_copy(0).wait_recv()

    @pl.when(corner_comes)
    def _():
        corner_send_copy().wait_recv()

    main = jnp.where(from_corner, corner[...], table[...]) * math.sqrt(head_dim)

    def place_bias(b, code):
        index = code - first_token
        index = jnp.where(index < 0, index + WIDE, jnp.where(index >= WIDE, index - WIDE, index))
        index = jnp.broadcast_to(jnp.clip(index, 0, WIDE - 1), (2 * heads, width))
        rows = []
        for t in range(half_t):
            a, at = divmod(WIDE * t, width)
            flat = index + at

            def take(k):
                tile = main[:, k * width : (k + 1) * width]
                return jnp.take_along_axis(
                    tile, flat & (width - 1), axis=1, mode="promise_in_bounds"
                )

            one = take(a)
            rows.append(one if at + WIDE <= width else jnp.where(flat < width, one, take(a + 1)))
        whole = jnp.concatenate(rows, axis=0)
        high = whole.astype(BF16)
        rest = whole - high.astype(F32)
        mid = rest.astype(BF16)
        rhs[b, pl.ds(width, used), :] = high
        rhs[b, pl.ds(2 * width, used), :] = mid
        rhs[b, pl.ds(3 * width, used), :] = (rest - mid.astype(F32)).astype(BF16)

    place_bias(0, codes0)
    place_bias(1, codes_a)
    place_bias(2, codes_b)
    log_scale = math.log2(math.e) / math.sqrt(head_dim)

    def attend(first_row, n_rows, which):
        both = lhs[pl.ds(first_row, heads * n_rows), :]
        hot = both[:, width:]
        left = jnp.concatenate([both, hot, hot], axis=1)
        scores = dot(left, jnp.concatenate([rhs[0], rhs[which]], axis=1))
        parts = []
        for h in range(heads):
            part = scores[h * n_rows : (h + 1) * n_rows]
            top = jnp.max(part, axis=1, keepdims=True)
            parts.append(jnp.exp2((part - top) * log_scale).astype(BF16))
        by_head = [vals[b, h] for h in range(heads) for b in (0, which)]
        mixed = dot(jnp.concatenate(parts, axis=1), jnp.concatenate(by_head, axis=0))
        return mixed[:, :width] / mixed[:, width:]

    out_a = attend(0, tail, 1)
    out_b = attend(heads * tail, margin, 2)
    attended = (gates * jnp.concatenate([out_a, out_b], axis=0)).astype(BF16)
    wo_copy.wait()
    new_atoms = (x_own.astype(F32) + dot(attended, wo[...])).astype(BF16)
    atoms_out[...] = new_atoms
    lifted = jnp.maximum(dot(new_atoms, wa_pad[...]), 0.0).astype(BF16)
    means = (dot(member, lifted) * inverse)[:tok_dev].astype(BF16)
    for c in range(n_col):
        tok_send[c] = means[:, c * width : c * width + share]

    def tok_copy(other):
        return pltpu.make_async_remote_copy(
            src_ref=tok_send.at[other],
            dst_ref=tok_recv.at[col],
            send_sem=tok_ssem,
            recv_sem=tok_rsem,
            device_id=(row, other),
            device_id_type=MESH,
        )

    for s in range(n_col - 1):
        tok_copy(nth(s)).start()
    tok_recv[col] = tok_send[col]
    others = pl.ds(0, n_col - 1)
    all_tokens = pltpu.make_async_remote_copy(
        src_ref=tok_send.at[others],
        dst_ref=tok_recv.at[others],
        send_sem=tok_ssem,
        recv_sem=tok_rsem,
        device_id=(row, (col + 1) % n_col),
        device_id_type=MESH,
    )
    all_tokens.wait_recv()

    all_tokens.wait_send()

    @pl.when(is_holder)
    def _():
        pltpu.make_async_remote_copy(
            src_ref=tsend.at[others],
            dst_ref=tsend.at[others],
            send_sem=table_send,
            recv_sem=table_recv,
            device_id=(row, (col + 1) % n_col),
            device_id_type=MESH,
        ).wait_send()

    @pl.when(corner_away)
    def _():
        corner_send_copy().wait_send()

    @pl.when(has_left)
    def _():
        for copy in to_left:
            copy.wait_send()

    @pl.when(has_right)
    def _():
        for copy in to_right:
            copy.wait_send()


def finish(atoms_ref, gathered, atoms_out, token_out, token_v, sems):
    atoms_copy = pltpu.make_async_copy(atoms_ref, atoms_out, sems.at[0])
    atoms_copy.start()
    rows = jnp.concatenate(
        [gathered[c].astype(F32) for c in range(gathered.shape[0])], axis=0
    )
    token_v[...] = rows.astype(BF16)
    token_copy = pltpu.make_async_copy(token_v, token_out, sems.at[1])
    token_copy.start()
    atoms_copy.wait()
    token_copy.wait()


def per_device(n_row, n_col, *args):
    x, pair, w_pair, w_query, w_keyval, w_gate, w_out, w_agg, tok, shift, mask = args
    w_pair = w_pair.T
    atoms, width = x.shape
    tok_rows, tok_cols, chan = pair.shape
    heads = w_pair.shape[0]
    tok_dev = tok_rows // n_col
    half_t = tok_dev // 2
    ct = w_agg.shape[1]
    margin = KW // 2
    lanes = -(-half_t * WIDE // 128) * 128
    hbm = pl.BlockSpec(memory_space=pltpu.HBM)
    vmem = pl.BlockSpec(memory_space=pltpu.VMEM)
    dma = pltpu.SemaphoreType.DMA
    scratch = [
        pltpu.VMEM((3 * width, width), BF16),
        pltpu.VMEM((n_col, half_t, 2 * WIDE, chan), BF16),
        pltpu.VMEM((half_t, 2 * WIDE, chan), BF16),
        pltpu.VMEM(w_pair.shape, BF16),
        pltpu.VMEM(w_query.shape, BF16),
        pltpu.VMEM(w_keyval.shape, BF16),
        pltpu.VMEM(w_gate.shape, BF16),
        pltpu.VMEM(w_out.shape, BF16),
        pltpu.VMEM(w_agg.shape, BF16),
        pltpu.VMEM((width, n_col * width), BF16),
        pltpu.VMEM(tok.shape, jnp.int32),
        pltpu.VMEM(mask.shape, jnp.int32),
        pltpu.SMEM(shift.shape, jnp.int32),
        pltpu.VMEM((n_col, 2 * heads, lanes), F32),
        pltpu.VMEM((2 * heads, lanes), F32),
        pltpu.VMEM((2 * heads, lanes), F32),
        pltpu.VMEM((2 * heads, lanes), F32),
        pltpu.VMEM((2, 8, width), jnp.int32),
        pltpu.VMEM((3, 8, width), jnp.int32),
        pltpu.VMEM((heads * atoms, 2 * width), BF16),
        pltpu.VMEM((3, 4 * width, width), BF16),
        pltpu.VMEM((3, heads, width, 2 * width), BF16),
        pltpu.VMEM((n_col, tok_dev, ct // n_col), BF16),
        dma((11,)),
        dma((n_col, 2)),
        dma((2,)),
        dma((4,)),
        dma((4,)),
        dma,
        dma,
        dma,
        dma,
        dma,
        dma,
    ]
    inputs = (x, pair, w_pair, w_query, w_keyval, w_gate, w_out, w_agg, tok, shift, mask)
    inputs = [pltpu.with_memory_space_constraint(a, pltpu.HBM) for a in inputs]
    new_atoms, gathered = pl.pallas_call(
        functools.partial(kernel, n_row, n_col),
        out_shape=(
            pltpu.VMEM((atoms, width), BF16),
            pltpu.VMEM((n_col, tok_dev, ct // n_col), BF16),
        ),
        in_specs=[hbm] * 11,
        out_specs=(vmem, vmem),
        scratch_shapes=scratch,
        compiler_params=pltpu.CompilerParams(
            collective_id=0, has_side_effects=True, vmem_limit_bytes=40 * 1024 * 1024
        ),
        name="atom_block",
    )(*inputs)
    return pl.pallas_call(
        finish,
        out_shape=(
            pltpu.HBM((atoms, width), BF16),
            pltpu.HBM((tok_rows, ct // n_col), BF16),
        ),
        in_specs=[vmem, vmem],
        out_specs=(hbm, hbm),
        scratch_shapes=[pltpu.VMEM((tok_rows, ct // n_col), BF16), dma((2,))],
        compiler_params=pltpu.CompilerParams(vmem_limit_bytes=8 * 1024 * 1024),
        name="write_out",
    )(new_atoms, gathered)


def solution(mesh):
    n_row, n_col = mesh.shape["row"], mesh.shape["col"]
    split = P(("row", "col"))
    in_specs = (
        P(("row", "col"), None),
        P("row", "col", None),
        P(),
        P(),
        P(),
        P(),
        P(),
        P(),
        split,
        split,
        split,
    )
    out_specs = (P(("row", "col"), None), P("row", "col"))
    return jax.shard_map(
        functools.partial(per_device, n_row, n_col),
        mesh=mesh,
        in_specs=in_specs,
        out_specs=out_specs,
        check_vma=False,
    )
```

```python
import functools
import math

import jax
import jax.numpy as jnp
from jax import lax
from jax.experimental import pallas as pl
from jax.experimental.pallas import tpu as pltpu
from jax.sharding import PartitionSpec as P

MESH = pl.DeviceIdType.MESH

QB = 32
KW = 128
WIDE = 72
OUTSIDE = -(2.0**126)
DEAD = -(2.0**100)
F32 = jnp.float32
BF16 = jnp.bfloat16


def dot(a, b):
    return jnp.dot(a, b, preferred_element_type=F32)


def dot_nt(a, b):
    return lax.dot_general(a, b, (((1,), (1,)), ((), ())), preferred_element_type=F32)


def kernel(
    n_row,
    n_col,
    x_in,
    pair_in,
    wp_in,
    wq_in,
    wkv_in,
    wg_in,
    wo_in,
    wa_in,
    tok_in,
    shift_in,
    mask_in,
    atoms_out,
    tok_recv,
    xs,
    strips,
    corner_x,
    wp,
    wq,
    wkv,
    wg,
    wo,
    wa,
    wa_pad,
    tok,
    mask,
    shift,
    tsend,
    csend,
    table,
    corner,
    messages,
    codes_s,
    lhs,
    rhs,
    vals,
    tok_send,
    in_sem,
    strip_sem,
    corner_sem,
    halo_send,
    halo_recv,
    table_send,
    table_recv,
    corner_send,
    corner_recv,
    tok_ssem,
    tok_rsem,
):
    row = lax.axis_index("row")
    col = lax.axis_index("col")
    me = row * n_col + col
    n_dev = n_row * n_col
    atoms, width = x_in.shape
    tok_rows, tok_cols, chan = pair_in.shape
    tok_dev = tok_rows // n_col
    half_t = tok_dev // 2
    heads = wp_in.shape[0]
    head_dim = width // heads
    margin = KW // 2
    per_col = tok_cols // tok_rows
    hold_col = row // per_col
    odd = row % per_col == per_col - 1
    even = row % per_col == 0
    is_holder = col == hold_col
    base = (row % per_col) * tok_rows
    has_left = me > 0
    has_right = me < n_dev - 1

    def nth(s):
        half = n_col // 2
        turn = (half // 2, 1, half - 1, 0)[s % half]
        side = col // half if s >= half else 1 - col // half
        return side * half + (col + turn) % half

    def strip_start(j):
        want = jnp.maximum(base + tok_dev * (j - 1), 0)
        return jnp.minimum(want, tok_cols - WIDE)

    barrier = pltpu.get_barrier_semaphore()

    for step in range(1, n_col):
        other = (col + step) % n_col
        pl.semaphore_signal(barrier, inc=1, device_id=(row, other), device_id_type=MESH)

    up_row = (col == 0) & has_left
    down_row = (col == n_col - 1) & has_right
    left_id = (jnp.where(col > 0, row, row - 1), (col + n_col - 1) % n_col)
    right_id = (jnp.where(col < n_col - 1, row, row + 1), (col + 1) % n_col)

    @pl.when(up_row)
    def _():
        pl.semaphore_signal(barrier, inc=1, device_id=left_id, device_id_type=MESH)

    @pl.when(down_row)
    def _():
        pl.semaphore_signal(barrier, inc=1, device_id=right_id, device_id_type=MESH)

    expected = n_col - 1 + up_row.astype(jnp.int32) + down_row.astype(jnp.int32)

    def local(i, src, dst):
        return pltpu.make_async_copy(src, dst, in_sem.at[i])

    tail = atoms - margin
    x_copy = local(0, x_in, xs.at[pl.ds(0, atoms)])
    tail_copy = local(1, x_in.at[pl.ds(tail, margin)], xs.at[pl.ds(2 * width, margin)])
    toks_copy = local(2, tok_in, tok)
    mask_copy = local(3, mask_in, mask)
    wp_copy = local(4, wp_in, wp)
    wq_copy = local(5, wq_in, wq)
    wg_copy = local(6, wg_in, wg)
    wkv_copy = local(7, wkv_in, wkv)
    shift_copy = local(8, shift_in, shift)
    wo_copy = local(9, wo_in, wo)
    wa_copy = local(10, wa_in, wa)

    def window_copies(first_row, first_col, dst, sems):
        return [
            pltpu.make_async_copy(
                pair_in.at[pl.ds(first_row + p * half_t, half_t), pl.ds(first_col, WIDE)],
                dst.at[:, pl.ds(p * WIDE, WIDE)],
                sems.at[p],
            )
            for p in range(2)
        ]

    def strip_copies(s):
        j = nth(s)
        start = pl.multiple_of(strip_start(j), 8)
        return window_copies(tok_dev * j, start, strips.at[s], strip_sem.at[s])

    x_copy.start()
    toks_copy.start()
    mask_copy.start()
    wp_copy.start()

    @pl.when(is_holder)
    def _():
        for s in range(n_col):
            for copy in strip_copies(s):
                copy.start()

    wq_copy.start()
    wg_copy.start()
    tail_copy.start()
    wkv_copy.start()
    shift_copy.start()
    wo_copy.start()
    wa_copy.start()

    corner_to = jnp.where(even, 0, n_col - 1)
    gives_corner = (even & (col == hold_col - 1)) | (odd & (col == hold_col + 1))
    takes_corner = (up_row & even) | (down_row & odd)
    corner_comes = takes_corner & jnp.logical_not(gives_corner)
    corner_away = gives_corner & jnp.logical_not(takes_corner)
    corner_col = pl.multiple_of(jnp.where(even, tok_cols - WIDE, 0), 8)
    corner_row = pl.multiple_of(jnp.where(even, 0, tok_rows - tok_dev), 8)
    corner_copies = window_copies(corner_row, corner_col, corner_x, corner_sem)

    @pl.when(gives_corner)
    def _():
        for copy in corner_copies:
            copy.start()

    @pl.when(jnp.logical_not(corner_comes))
    def _():
        corner[...] = jnp.zeros_like(corner)

    def project(block):
        w_one = wp[...].astype(F32)
        w_rows = jnp.concatenate([w_one, w_one], axis=0)
        first_half = lax.broadcasted_iota(jnp.int32, w_rows.shape, 0) < heads
        w_both = jnp.concatenate(
            [jnp.where(first_half, w_rows, 0.0), jnp.where(first_half, 0.0, w_rows)], axis=1
        ).astype(BF16)
        flat = block.reshape(tok_dev * WIDE, chan)
        low, high = flat[: half_t * WIDE], flat[half_t * WIDE :]
        out = dot_nt(w_both, jnp.concatenate([low, high], axis=1))
        spare = table.shape[1] - out.shape[1]
        return jnp.concatenate([out, jnp.zeros((2 * heads, spare), F32)], axis=1)

    def corner_send_copy():
        return pltpu.make_async_remote_copy(
            src_ref=csend,
            dst_ref=corner,
            send_sem=corner_send,
            recv_sem=corner_recv,
            device_id=(row, corner_to),
            device_id_type=MESH,
        )

    def table_send_copy(s):
        j = nth(s)
        return pltpu.make_async_remote_copy(
            src_ref=tsend.at[s],
            dst_ref=table,
            send_sem=table_send,
            recv_sem=table_recv,
            device_id=(row, j),
            device_id_type=MESH,
        )

    toks_copy.wait()
    mask_copy.wait()
    spare = 2 * width - atoms
    tokens = jnp.concatenate(
        [tok[...].reshape(1, atoms), jnp.full((1, spare), -1, jnp.int32)], axis=1
    )
    masks = jnp.concatenate(
        [mask[...].reshape(1, atoms), jnp.zeros((1, spare), jnp.int32)], axis=1
    )
    codes = jnp.where(masks == 1, tokens, -1)
    codes0, codes1 = codes[:, :width], codes[:, width:]
    messages[0] = jnp.broadcast_to(pltpu.roll(codes0, margin, 1), (8, width))
    messages[1] = jnp.broadcast_to(pltpu.roll(codes1, margin, 1), (8, width))

    def halo(i, src, dst, device):
        return pltpu.make_async_remote_copy(
            src_ref=src,
            dst_ref=dst,
            send_sem=halo_send.at[i],
            recv_sem=halo_recv.at[i],
            device_id=device,
            device_id_type=MESH,
        )

    x_left, x_right = pl.ds(atoms, margin), pl.ds(2 * width + margin, margin)
    to_left = (
        halo(0, xs.at[pl.ds(0, margin)], xs.at[x_right], left_id),
        halo(1, messages.at[0], codes_s.at[2], left_id),
    )
    to_right = (
        halo(2, xs.at[pl.ds(tail, margin)], xs.at[x_left], right_id),
        halo(3, messages.at[1], codes_s.at[1], right_id),
    )

    @pl.when(jnp.logical_not(has_left))
    def _():
        xs[x_left] = jnp.zeros((margin, width), BF16)
        codes_s[1] = jnp.full((8, width), -1, jnp.int32)

    @pl.when(jnp.logical_not(has_right))
    def _():
        xs[x_right] = jnp.zeros((margin, width), BF16)
        codes_s[2] = jnp.full((8, width), -1, jnp.int32)

    x_copy.wait()

    def send_halos():
        @pl.when(has_left)
        def _():
            for copy in to_left:
                copy.start()

        @pl.when(has_right)
        def _():
            for copy in to_right:
                copy.start()

    comes_last = col == n_col - 1

    @pl.when(jnp.logical_not(is_holder) & comes_last)
    def _():
        pl.semaphore_wait(barrier, expected)
        send_halos()

    used = 2 * heads * half_t
    wq_copy.wait()
    wg_copy.wait()
    wkv_copy.wait()
    shift_copy.wait()
    x_own = xs[pl.ds(0, atoms)]
    queries = dot(x_own, wq[...])
    gates = jax.nn.sigmoid(dot(x_own, wg[...]))
    lanes = lax.broadcasted_iota(jnp.int32, (atoms, width), 1)
    local_tok = tokens - tok_dev * me
    second = (local_tok >= half_t).astype(jnp.int32)
    within = local_tok - half_t * second
    lower = (within >= half_t // 2).astype(jnp.int32)
    place = 2 * heads * (2 * within - half_t * lower + second) + heads * lower
    place = jnp.transpose(jnp.broadcast_to(place, (width, 2 * width)))[:atoms]
    mark = used + lax.broadcasted_iota(jnp.int32, (atoms, width), 0) // QB
    for h in range(heads):
        q_h = jnp.where(lanes // head_dim == h, queries, 0.0).astype(BF16)
        hot_h = ((lanes == place + h) | (lanes == mark)).astype(F32).astype(BF16)
        low, high = pl.ds(h * tail, tail), pl.ds(heads * tail + h * margin, margin)
        lhs[low, pl.ds(0, width)] = q_h[:tail]
        lhs[low, pl.ds(width, width)] = hot_h[:tail]
        lhs[high, pl.ds(0, width)] = q_h[tail:]
        lhs[high, pl.ds(width, width)] = hot_h[tail:]
    wa_copy.wait()
    share = wa_in.shape[1] // n_col
    for c in range(n_col):
        wa_pad[:, c * width : (c + 1) * width] = jnp.concatenate(
            [wa[:, c * share : (c + 1) * share], jnp.zeros((width, width - share), BF16)], axis=1
        )
    member = lax.broadcasted_iota(jnp.int32, (32, atoms), 0) == (codes - tok_dev * me)[:, :atoms]
    member = member.astype(F32)
    count = jnp.sum(member, axis=1, keepdims=True)
    inverse = 1.0 / jnp.maximum(count, 1.0)
    member = member.astype(BF16)

    head_of = lax.broadcasted_iota(jnp.int32, (width, width), 1) // head_dim

    def place_keyval(b, keyval):
        rhs[b, pl.ds(0, width), :] = jnp.transpose(keyval[:, :width]).astype(BF16)
        for h in range(heads):
            vals[b, h, :, pl.ds(0, width)] = jnp.where(
                head_of == h, keyval[:, width:], 0.0
            ).astype(BF16)

    for h in range(heads):
        mine = (head_of == h).astype(F32).astype(BF16)
        for b in range(3):
            vals[b, h, :, pl.ds(width, width)] = mine

    place_keyval(0, dot(xs[pl.ds(0, width)], wkv[...]))
    side = lax.broadcasted_iota(jnp.int32, (1, width), 1)
    rest_rows = width - used
    sub = lax.broadcasted_iota(jnp.int32, (rest_rows, width), 0)
    starts = jnp.zeros((rest_rows, width), jnp.int32)
    n_blocks = atoms // QB
    for b in range(n_blocks):
        starts = jnp.where(sub == b, QB * b - KW // 2 + QB // 2 + shift[b], starts)

    def place_mask(b, at, code):
        inside = (at >= starts) & (at < starts + KW)
        value = jnp.where(inside, jnp.where(code >= 0, 0.0, DEAD), OUTSIDE)
        rhs[b, pl.ds(width + used, rest_rows), :] = jnp.where(sub < n_blocks, value, 0.0).astype(
            BF16
        )
        for k in (2, 3):
            rhs[b, pl.ds(k * width + used, rest_rows), :] = jnp.zeros((rest_rows, width), BF16)

    place_mask(0, side, codes0)
    @pl.when(jnp.logical_not(is_holder | comes_last))
    def _():
        pl.semaphore_wait(barrier, expected)
        send_halos()

    @pl.when(gives_corner)
    def _():
        wp_copy.wait()
        for copy in corner_copies:
            copy.wait()
        csend[...] = project(corner_x[...])

    @pl.when(corner_away)
    def _():
        corner_send_copy().start()

    @pl.when(gives_corner & takes_corner)
    def _():
        corner[...] = csend[...]

    group = n_col // 2
    starts_early = hold_col % group < group // 2

    def announce():
        pl.semaphore_wait(barrier, expected)
        for s in range(group):
            table_send_copy(s).start()
        send_halos()

    @pl.when(is_holder)
    def _():
        wp_copy.wait()
        for begin in range(0, n_col, group):
            for s in range(begin, begin + group):
                for copy in strip_copies(s):
                    copy.wait()
            for s in range(begin, begin + group):
                tsend[s] = project(strips[s])
            pl.when(starts_early == (begin > 0))(announce)
        for s in range(group, n_col - 1):
            table_send_copy(s).start()
        table[...] = tsend[n_col - 1]

    @pl.when(jnp.logical_not(is_holder | gives_corner))
    def _():
        wp_copy.wait()

    tail_copy.wait()

    @pl.when(has_left)
    def _():
        for copy in to_right:
            copy.wait_recv()

    @pl.when(has_right)
    def _():
        for copy in to_left:
            copy.wait_recv()

    keyval = dot(xs[pl.ds(width, 2 * width)], wkv[...])
    place_keyval(1, keyval[:width])
    place_keyval(2, keyval[width:])
    codes_a = jnp.where(side < margin, codes1, codes_s[1][0:1])
    codes_b = jnp.where(side < margin, codes1, codes_s[2][0:1])
    place_mask(1, jnp.where(side < margin, side + width, side - width), codes_a)
    place_mask(2, side + width, codes_b)

    first_token = hold_col * tok_cols + strip_start(col)
    in_strip = lax.broadcasted_iota(jnp.int32, table.shape, 1) % WIDE
    from_low = in_strip >= jnp.where(takes_corner & even, WIDE - tok_dev, WIDE)
    from_high = in_strip < jnp.where(takes_corner & odd, tok_dev, 0)
    from_corner = from_low | from_high

    @pl.when(jnp.logical_not(is_holder))
    def _():
        table_send_copy(0).wait_recv()

    @pl.when(corner_comes)
    def _():
        corner_send_copy().wait_recv()

    main = jnp.where(from_corner, corner[...], table[...]) * math.sqrt(head_dim)

    def place_bias(b, code):
        index = code - first_token
        index = jnp.where(index < 0, index + WIDE, jnp.where(index >= WIDE, index - WIDE, index))
        index = jnp.broadcast_to(jnp.clip(index, 0, WIDE - 1), (2 * heads, width))
        rows = []
        for t in range(half_t):
            a, at = divmod(WIDE * t, width)
            flat = index + at

            def take(k):
                tile = main[:, k * width : (k + 1) * width]
                return jnp.take_along_axis(
                    tile, flat & (width - 1), axis=1, mode="promise_in_bounds"
                )

            one = take(a)
            rows.append(one if at + WIDE <= width else jnp.where(flat < width, one, take(a + 1)))
        whole = jnp.concatenate(rows, axis=0)
        high = whole.astype(BF16)
        rest = whole - high.astype(F32)
        mid = rest.astype(BF16)
        rhs[b, pl.ds(width, used), :] = high
        rhs[b, pl.ds(2 * width, used), :] = mid
        rhs[b, pl.ds(3 * width, used), :] = (rest - mid.astype(F32)).astype(BF16)

    place_bias(0, codes0)
    place_bias(1, codes_a)
    place_bias(2, codes_b)
    log_scale = math.log2(math.e) / math.sqrt(head_dim)

    def attend(first_row, n_rows, which):
        both = lhs[pl.ds(first_row, heads * n_rows), :]
        hot = both[:, width:]
        left = jnp.concatenate([both, hot, hot], axis=1)
        scores = dot(left, jnp.concatenate([rhs[0], rhs[which]], axis=1))
        parts = []
        for h in range(heads):
            part = scores[h * n_rows : (h + 1) * n_rows]
            top = jnp.max(part, axis=1, keepdims=True)
            parts.append(jnp.exp2((part - top) * log_scale).astype(BF16))
        by_head = [vals[b, h] for h in range(heads) for b in (0, which)]
        mixed = dot(jnp.concatenate(parts, axis=1), jnp.concatenate(by_head, axis=0))
        return mixed[:, :width] / mixed[:, width:]

    out_a = attend(0, tail, 1)
    out_b = attend(heads * tail, margin, 2)
    attended = (gates * jnp.concatenate([out_a, out_b], axis=0)).astype(BF16)
    wo_copy.wait()
    new_atoms = (x_own.astype(F32) + dot(attended, wo[...])).astype(BF16)
    atoms_out[...] = new_atoms
    lifted = jnp.maximum(dot(new_atoms, wa_pad[...]), 0.0).astype(BF16)
    means = (dot(member, lifted) * inverse)[:tok_dev].astype(BF16)
    for c in range(n_col):
        tok_send[c] = means[:, c * width : c * width + share]

    def tok_copy(other):
        return pltpu.make_async_remote_copy(
            src_ref=tok_send.at[other],
            dst_ref=tok_recv.at[col],
            send_sem=tok_ssem,
            recv_sem=tok_rsem,
            device_id=(row, other),
            device_id_type=MESH,
        )

    for s in range(n_col - 1):
        tok_copy(nth(s)).start()
    tok_recv[col] = tok_send[col]
    others = pl.ds(0, n_col - 1)
    all_tokens = pltpu.make_async_remote_copy(
        src_ref=tok_send.at[others],
        dst_ref=tok_recv.at[others],
        send_sem=tok_ssem,
        recv_sem=tok_rsem,
        device_id=(row, (col + 1) % n_col),
        device_id_type=MESH,
    )
    all_tokens.wait_recv()

    all_tokens.wait_send()

    @pl.when(is_holder)
    def _():
        pltpu.make_async_remote_copy(
            src_ref=tsend.at[others],
            dst_ref=tsend.at[others],
            send_sem=table_send,
            recv_sem=table_recv,
            device_id=(row, (col + 1) % n_col),
            device_id_type=MESH,
        ).wait_send()

    @pl.when(corner_away)
    def _():
        corner_send_copy().wait_send()

    @pl.when(has_left)
    def _():
        for copy in to_left:
            copy.wait_send()

    @pl.when(has_right)
    def _():
        for copy in to_right:
            copy.wait_send()


def finish(atoms_ref, gathered, atoms_out, token_out, token_v, sems):
    atoms_copy = pltpu.make_async_copy(atoms_ref, atoms_out, sems.at[0])
    atoms_copy.start()
    rows = jnp.concatenate(
        [gathered[c].astype(F32) for c in range(gathered.shape[0])], axis=0
    )
    token_v[...] = rows.astype(BF16)
    token_copy = pltpu.make_async_copy(token_v, token_out, sems.at[1])
    token_copy.start()
    atoms_copy.wait()
    token_copy.wait()


def per_device(n_row, n_col, *args):
    x, pair, w_pair, w_query, w_keyval, w_gate, w_out, w_agg, tok, shift, mask = args
    w_pair = w_pair.T
    atoms, width = x.shape
    tok_rows, tok_cols, chan = pair.shape
    heads = w_pair.shape[0]
    tok_dev = tok_rows // n_col
    half_t = tok_dev // 2
    ct = w_agg.shape[1]
    margin = KW // 2
    lanes = -(-half_t * WIDE // 128) * 128
    hbm = pl.BlockSpec(memory_space=pltpu.HBM)
    vmem = pl.BlockSpec(memory_space=pltpu.VMEM)
    dma = pltpu.SemaphoreType.DMA
    scratch = [
        pltpu.VMEM((3 * width, width), BF16),
        pltpu.VMEM((n_col, half_t, 2 * WIDE, chan), BF16),
        pltpu.VMEM((half_t, 2 * WIDE, chan), BF16),
        pltpu.VMEM(w_pair.shape, BF16),
        pltpu.VMEM(w_query.shape, BF16),
        pltpu.VMEM(w_keyval.shape, BF16),
        pltpu.VMEM(w_gate.shape, BF16),
        pltpu.VMEM(w_out.shape, BF16),
        pltpu.VMEM(w_agg.shape, BF16),
        pltpu.VMEM((width, n_col * width), BF16),
        pltpu.VMEM(tok.shape, jnp.int32),
        pltpu.VMEM(mask.shape, jnp.int32),
        pltpu.SMEM(shift.shape, jnp.int32),
        pltpu.VMEM((n_col, 2 * heads, lanes), F32),
        pltpu.VMEM((2 * heads, lanes), F32),
        pltpu.VMEM((2 * heads, lanes), F32),
        pltpu.VMEM((2 * heads, lanes), F32),
        pltpu.VMEM((2, 8, width), jnp.int32),
        pltpu.VMEM((3, 8, width), jnp.int32),
        pltpu.VMEM((heads * atoms, 2 * width), BF16),
        pltpu.VMEM((3, 4 * width, width), BF16),
        pltpu.VMEM((3, heads, width, 2 * width), BF16),
        pltpu.VMEM((n_col, tok_dev, ct // n_col), BF16),
        dma((11,)),
        dma((n_col, 2)),
        dma((2,)),
        dma((4,)),
        dma((4,)),
        dma,
        dma,
        dma,
        dma,
        dma,
        dma,
    ]
    inputs = (x, pair, w_pair, w_query, w_keyval, w_gate, w_out, w_agg, tok, shift, mask)
    inputs = [pltpu.with_memory_space_constraint(a, pltpu.HBM) for a in inputs]
    new_atoms, gathered = pl.pallas_call(
        functools.partial(kernel, n_row, n_col),
        out_shape=(
            pltpu.VMEM((atoms, width), BF16),
            pltpu.VMEM((n_col, tok_dev, ct // n_col), BF16),
        ),
        in_specs=[hbm] * 11,
        out_specs=(vmem, vmem),
        scratch_shapes=scratch,
        compiler_params=pltpu.CompilerParams(
            collective_id=0, has_side_effects=True, vmem_limit_bytes=40 * 1024 * 1024
        ),
        name="atom_block",
    )(*inputs)
    return pl.pallas_call(
        finish,
        out_shape=(
            pltpu.HBM((atoms, width), BF16),
            pltpu.HBM((tok_rows, ct // n_col), BF16),
        ),
        in_specs=[vmem, vmem],
        out_specs=(hbm, hbm),
        scratch_shapes=[pltpu.VMEM((tok_rows, ct // n_col), BF16), dma((2,))],
        compiler_params=pltpu.CompilerParams(vmem_limit_bytes=8 * 1024 * 1024),
        name="write_out",
    )(new_atoms, gathered)


def solution(mesh):
    n_row, n_col = mesh.shape["row"], mesh.shape["col"]
    split = P(("row", "col"))
    in_specs = (
        P(("row", "col"), None),
        P("row", "col", None),
        P(),
        P(),
        P(),
        P(),
        P(),
        P(),
        split,
        split,
        split,
    )
    out_specs = (P(("row", "col"), None), P("row", "col"))
    return jax.shard_map(
        functools.partial(per_device, n_row, n_col),
        mesh=mesh,
        in_specs=in_specs,
        out_specs=out_specs,
        check_vma=False,
    )
```

```python
import functools
import math

import jax
import jax.numpy as jnp
from jax import lax
from jax.experimental import pallas as pl
from jax.experimental.pallas import tpu as pltpu
from jax.sharding import PartitionSpec as P

MESH = pl.DeviceIdType.MESH

QB = 32
KW = 128
WIDE = 72
OUTSIDE = -(2.0**126)
DEAD = -(2.0**100)
F32 = jnp.float32
BF16 = jnp.bfloat16


def dot(a, b):
    return jnp.dot(a, b, preferred_element_type=F32)


def dot_nt(a, b):
    return lax.dot_general(a, b, (((1,), (1,)), ((), ())), preferred_element_type=F32)


def kernel(
    n_row,
    n_col,
    x_in,
    pair_in,
    wp_in,
    wq_in,
    wkv_in,
    wg_in,
    wo_in,
    wa_in,
    tok_in,
    shift_in,
    mask_in,
    atoms_out,
    tok_recv,
    xs,
    strips,
    corner_x,
    wp,
    wq,
    wkv,
    wg,
    wo,
    wa,
    wa_pad,
    tok,
    mask,
    shift,
    tsend,
    csend,
    table,
    corner,
    messages,
    codes_s,
    lhs,
    rhs,
    vals,
    tok_send,
    in_sem,
    strip_sem,
    corner_sem,
    halo_send,
    halo_recv,
    table_send,
    table_recv,
    corner_send,
    corner_recv,
    tok_ssem,
    tok_rsem,
):
    row = lax.axis_index("row")
    col = lax.axis_index("col")
    me = row * n_col + col
    n_dev = n_row * n_col
    atoms, width = x_in.shape
    tok_rows, tok_cols, chan = pair_in.shape
    tok_dev = tok_rows // n_col
    half_t = tok_dev // 2
    heads = wp_in.shape[0]
    head_dim = width // heads
    margin = KW // 2
    per_col = tok_cols // tok_rows
    hold_col = row // per_col
    odd = row % per_col == per_col - 1
    even = row % per_col == 0
    is_holder = col == hold_col
    base = (row % per_col) * tok_rows
    has_left = me > 0
    has_right = me < n_dev - 1

    def nth(s):
        half = n_col // 2
        turn = (half // 2, 1, half - 1, 0)[s % half]
        side = col // half if s >= half else 1 - col // half
        return side * half + (col + turn) % half

    def strip_start(j):
        want = jnp.maximum(base + tok_dev * (j - 1), 0)
        return jnp.minimum(want, tok_cols - WIDE)

    barrier = pltpu.get_barrier_semaphore()

    for step in range(1, n_col):
        other = (col + step) % n_col
        pl.semaphore_signal(barrier, inc=1, device_id=(row, other), device_id_type=MESH)

    up_row = (col == 0) & has_left
    down_row = (col == n_col - 1) & has_right
    left_id = (jnp.where(col > 0, row, row - 1), (col + n_col - 1) % n_col)
    right_id = (jnp.where(col < n_col - 1, row, row + 1), (col + 1) % n_col)

    @pl.when(up_row)
    def _():
        pl.semaphore_signal(barrier, inc=1, device_id=left_id, device_id_type=MESH)

    @pl.when(down_row)
    def _():
        pl.semaphore_signal(barrier, inc=1, device_id=right_id, device_id_type=MESH)

    expected = n_col - 1 + up_row.astype(jnp.int32) + down_row.astype(jnp.int32)

    def local(i, src, dst):
        return pltpu.make_async_copy(src, dst, in_sem.at[i])

    tail = atoms - margin
    x_copy = local(0, x_in, xs.at[pl.ds(0, atoms)])
    tail_copy = local(1, x_in.at[pl.ds(tail, margin)], xs.at[pl.ds(2 * width, margin)])
    toks_copy = local(2, tok_in, tok)
    mask_copy = local(3, mask_in, mask)
    wp_copy = local(4, wp_in, wp)
    wq_copy = local(5, wq_in, wq)
    wg_copy = local(6, wg_in, wg)
    wkv_copy = local(7, wkv_in, wkv)
    shift_copy = local(8, shift_in, shift)
    wo_copy = local(9, wo_in, wo)
    wa_copy = local(10, wa_in, wa)

    def window_copies(first_row, first_col, dst, sems):
        return [
            pltpu.make_async_copy(
                pair_in.at[pl.ds(first_row + p * half_t, half_t), pl.ds(first_col, WIDE)],
                dst.at[:, pl.ds(p * WIDE, WIDE)],
                sems.at[p],
            )
            for p in range(2)
        ]

    def strip_copies(s):
        j = nth(s)
        start = pl.multiple_of(strip_start(j), 8)
        return window_copies(tok_dev * j, start, strips.at[s], strip_sem.at[s])

    x_copy.start()
    toks_copy.start()
    mask_copy.start()
    wp_copy.start()

    @pl.when(is_holder)
    def _():
        for s in range(n_col):
            for copy in strip_copies(s):
                copy.start()

    wq_copy.start()
    wg_copy.start()
    tail_copy.start()
    wkv_copy.start()
    shift_copy.start()
    wo_copy.start()
    wa_copy.start()

    corner_to = jnp.where(even, 0, n_col - 1)
    gives_corner = (even & (col == hold_col - 1)) | (odd & (col == hold_col + 1))
    takes_corner = (up_row & even) | (down_row & odd)
    corner_comes = takes_corner & jnp.logical_not(gives_corner)
    corner_away = gives_corner & jnp.logical_not(takes_corner)
    corner_col = pl.multiple_of(jnp.where(even, tok_cols - WIDE, 0), 8)
    corner_row = pl.multiple_of(jnp.where(even, 0, tok_rows - tok_dev), 8)
    corner_copies = window_copies(corner_row, corner_col, corner_x, corner_sem)

    @pl.when(gives_corner)
    def _():
        for copy in corner_copies:
            copy.start()

    @pl.when(jnp.logical_not(corner_comes))
    def _():
        corner[...] = jnp.zeros_like(corner)

    def project(block):
        w_one = wp[...].astype(F32)
        w_rows = jnp.concatenate([w_one, w_one], axis=0)
        first_half = lax.broadcasted_iota(jnp.int32, w_rows.shape, 0) < heads
        w_both = jnp.concatenate(
            [jnp.where(first_half, w_rows, 0.0), jnp.where(first_half, 0.0, w_rows)], axis=1
        ).astype(BF16)
        flat = block.reshape(tok_dev * WIDE, chan)
        low, high = flat[: half_t * WIDE], flat[half_t * WIDE :]
        out = dot_nt(w_both, jnp.concatenate([low, high], axis=1))
        spare = table.shape[1] - out.shape[1]
        return jnp.concatenate([out, jnp.zeros((2 * heads, spare), F32)], axis=1)

    def corner_send_copy():
        return pltpu.make_async_remote_copy(
            src_ref=csend,
            dst_ref=corner,
            send_sem=corner_send,
            recv_sem=corner_recv,
            device_id=(row, corner_to),
            device_id_type=MESH,
        )

    def table_send_copy(s):
        j = nth(s)
        return pltpu.make_async_remote_copy(
            src_ref=tsend.at[s],
            dst_ref=table,
            send_sem=table_send,
            recv_sem=table_recv,
            device_id=(row, j),
            device_id_type=MESH,
        )

    toks_copy.wait()
    mask_copy.wait()
    spare = 2 * width - atoms
    tokens = jnp.concatenate(
        [tok[...].reshape(1, atoms), jnp.full((1, spare), -1, jnp.int32)], axis=1
    )
    masks = jnp.concatenate(
        [mask[...].reshape(1, atoms), jnp.zeros((1, spare), jnp.int32)], axis=1
    )
    codes = jnp.where(masks == 1, tokens, -1)
    codes0, codes1 = codes[:, :width], codes[:, width:]
    messages[0] = jnp.broadcast_to(pltpu.roll(codes0, margin, 1), (8, width))
    messages[1] = jnp.broadcast_to(pltpu.roll(codes1, margin, 1), (8, width))

    def halo(i, src, dst, device):
        return pltpu.make_async_remote_copy(
            src_ref=src,
            dst_ref=dst,
            send_sem=halo_send.at[i],
            recv_sem=halo_recv.at[i],
            device_id=device,
            device_id_type=MESH,
        )

    x_left, x_right = pl.ds(atoms, margin), pl.ds(2 * width + margin, margin)
    to_left = (
        halo(0, xs.at[pl.ds(0, margin)], xs.at[x_right], left_id),
        halo(1, messages.at[0], codes_s.at[2], left_id),
    )
    to_right = (
        halo(2, xs.at[pl.ds(tail, margin)], xs.at[x_left], right_id),
        halo(3, messages.at[1], codes_s.at[1], right_id),
    )

    @pl.when(jnp.logical_not(has_left))
    def _():
        xs[x_left] = jnp.zeros((margin, width), BF16)
        codes_s[1] = jnp.full((8, width), -1, jnp.int32)

    @pl.when(jnp.logical_not(has_right))
    def _():
        xs[x_right] = jnp.zeros((margin, width), BF16)
        codes_s[2] = jnp.full((8, width), -1, jnp.int32)

    x_copy.wait()

    def send_halos():
        @pl.when(has_right)
        def _():
            for copy in to_right:
                copy.start()

        @pl.when(has_left)
        def _():
            for copy in to_left:
                copy.start()

    comes_last = col == n_col - 1

    @pl.when(jnp.logical_not(is_holder) & comes_last)
    def _():
        pl.semaphore_wait(barrier, expected)
        send_halos()

    used = 2 * heads * half_t
    wq_copy.wait()
    wg_copy.wait()
    wkv_copy.wait()
    shift_copy.wait()
    x_own = xs[pl.ds(0, atoms)]
    queries = dot(x_own, wq[...])
    gates = jax.nn.sigmoid(dot(x_own, wg[...]))
    lanes = lax.broadcasted_iota(jnp.int32, (atoms, width), 1)
    local_tok = tokens - tok_dev * me
    second = (local_tok >= half_t).astype(jnp.int32)
    within = local_tok - half_t * second
    lower = (within >= half_t // 2).astype(jnp.int32)
    place = 2 * heads * (2 * within - half_t * lower + second) + heads * lower
    place = jnp.transpose(jnp.broadcast_to(place, (width, 2 * width)))[:atoms]
    mark = used + lax.broadcasted_iota(jnp.int32, (atoms, width), 0) // QB
    for h in range(heads):
        q_h = jnp.where(lanes // head_dim == h, queries, 0.0).astype(BF16)
        hot_h = ((lanes == place + h) | (lanes == mark)).astype(F32).astype(BF16)
        low, high = pl.ds(h * tail, tail), pl.ds(heads * tail + h * margin, margin)
        lhs[low, pl.ds(0, width)] = q_h[:tail]
        lhs[low, pl.ds(width, width)] = hot_h[:tail]
        lhs[high, pl.ds(0, width)] = q_h[tail:]
        lhs[high, pl.ds(width, width)] = hot_h[tail:]
    wa_copy.wait()
    share = wa_in.shape[1] // n_col
    for c in range(n_col):
        wa_pad[:, c * width : (c + 1) * width] = jnp.concatenate(
            [wa[:, c * share : (c + 1) * share], jnp.zeros((width, width - share), BF16)], axis=1
        )
    member = lax.broadcasted_iota(jnp.int32, (32, atoms), 0) == (codes - tok_dev * me)[:, :atoms]
    member = member.astype(F32)
    count = jnp.sum(member, axis=1, keepdims=True)
    inverse = 1.0 / jnp.maximum(count, 1.0)
    member = member.astype(BF16)

    head_of = lax.broadcasted_iota(jnp.int32, (width, width), 1) // head_dim

    def place_keyval(b, keyval):
        rhs[b, pl.ds(0, width), :] = jnp.transpose(keyval[:, :width]).astype(BF16)
        for h in range(heads):
            vals[b, h, :, pl.ds(0, width)] = jnp.where(
                head_of == h, keyval[:, width:], 0.0
            ).astype(BF16)

    for h in range(heads):
        mine = (head_of == h).astype(F32).astype(BF16)
        for b in range(3):
            vals[b, h, :, pl.ds(width, width)] = mine

    place_keyval(0, dot(xs[pl.ds(0, width)], wkv[...]))
    side = lax.broadcasted_iota(jnp.int32, (1, width), 1)
    rest_rows = width - used
    sub = lax.broadcasted_iota(jnp.int32, (rest_rows, width), 0)
    starts = jnp.zeros((rest_rows, width), jnp.int32)
    n_blocks = atoms // QB
    for b in range(n_blocks):
        starts = jnp.where(sub == b, QB * b - KW // 2 + QB // 2 + shift[b], starts)

    def place_mask(b, at, code):
        inside = (at >= starts) & (at < starts + KW)
        value = jnp.where(inside, jnp.where(code >= 0, 0.0, DEAD), OUTSIDE)
        rhs[b, pl.ds(width + used, rest_rows), :] = jnp.where(sub < n_blocks, value, 0.0).astype(
            BF16
        )
        for k in (2, 3):
            rhs[b, pl.ds(k * width + used, rest_rows), :] = jnp.zeros((rest_rows, width), BF16)

    place_mask(0, side, codes0)
    @pl.when(jnp.logical_not(is_holder | comes_last))
    def _():
        pl.semaphore_wait(barrier, expected)
        send_halos()

    @pl.when(gives_corner)
    def _():
        wp_copy.wait()
        for copy in corner_copies:
            copy.wait()
        csend[...] = project(corner_x[...])

    @pl.when(corner_away)
    def _():
        corner_send_copy().start()

    @pl.when(gives_corner & takes_corner)
    def _():
        corner[...] = csend[...]

    group = n_col // 2
    starts_early = hold_col % group < group // 2

    def announce():
        pl.semaphore_wait(barrier, expected)
        for s in range(group):
            table_send_copy(s).start()
        send_halos()

    @pl.when(is_holder)
    def _():
        wp_copy.wait()
        for begin in range(0, n_col, group):
            for s in range(begin, begin + group):
                for copy in strip_copies(s):
                    copy.wait()
            for s in range(begin, begin + group):
                tsend[s] = project(strips[s])
            pl.when(starts_early == (begin > 0))(announce)
        for s in range(group, n_col - 1):
            table_send_copy(s).start()
        table[...] = tsend[n_col - 1]

    @pl.when(jnp.logical_not(is_holder | gives_corner))
    def _():
        wp_copy.wait()

    tail_copy.wait()

    @pl.when(has_left)
    def _():
        for copy in to_right:
            copy.wait_recv()

    @pl.when(has_right)
    def _():
        for copy in to_left:
            copy.wait_recv()

    keyval = dot(xs[pl.ds(width, 2 * width)], wkv[...])
    place_keyval(1, keyval[:width])
    place_keyval(2, keyval[width:])
    codes_a = jnp.where(side < margin, codes1, codes_s[1][0:1])
    codes_b = jnp.where(side < margin, codes1, codes_s[2][0:1])
    place_mask(1, jnp.where(side < margin, side + width, side - width), codes_a)
    place_mask(2, side + width, codes_b)

    first_token = hold_col * tok_cols + strip_start(col)
    in_strip = lax.broadcasted_iota(jnp.int32, table.shape, 1) % WIDE
    from_low = in_strip >= jnp.where(takes_corner & even, WIDE - tok_dev, WIDE)
    from_high = in_strip < jnp.where(takes_corner & odd, tok_dev, 0)
    from_corner = from_low | from_high

    @pl.when(jnp.logical_not(is_holder))
    def _():
        table_send_copy(0).wait_recv()

    @pl.when(corner_comes)
    def _():
        corner_send_copy().wait_recv()

    main = jnp.where(from_corner, corner[...], table[...]) * math.sqrt(head_dim)

    def place_bias(b, code):
        index = code - first_token
        index = jnp.where(index < 0, index + WIDE, jnp.where(index >= WIDE, index - WIDE, index))
        index = jnp.broadcast_to(jnp.clip(index, 0, WIDE - 1), (2 * heads, width))
        rows = []
        for t in range(half_t):
            a, at = divmod(WIDE * t, width)
            flat = index + at

            def take(k):
                tile = main[:, k * width : (k + 1) * width]
                return jnp.take_along_axis(
                    tile, flat & (width - 1), axis=1, mode="promise_in_bounds"
                )

            one = take(a)
            rows.append(one if at + WIDE <= width else jnp.where(flat < width, one, take(a + 1)))
        whole = jnp.concatenate(rows, axis=0)
        high = whole.astype(BF16)
        rest = whole - high.astype(F32)
        mid = rest.astype(BF16)
        rhs[b, pl.ds(width, used), :] = high
        rhs[b, pl.ds(2 * width, used), :] = mid
        rhs[b, pl.ds(3 * width, used), :] = (rest - mid.astype(F32)).astype(BF16)

    place_bias(0, codes0)
    place_bias(1, codes_a)
    place_bias(2, codes_b)
    log_scale = math.log2(math.e) / math.sqrt(head_dim)

    def attend(first_row, n_rows, which):
        both = lhs[pl.ds(first_row, heads * n_rows), :]
        hot = both[:, width:]
        left = jnp.concatenate([both, hot, hot], axis=1)
        scores = dot(left, jnp.concatenate([rhs[0], rhs[which]], axis=1))
        parts = []
        for h in range(heads):
            part = scores[h * n_rows : (h + 1) * n_rows]
            top = jnp.max(part, axis=1, keepdims=True)
            parts.append(jnp.exp2((part - top) * log_scale).astype(BF16))
        by_head = [vals[b, h] for h in range(heads) for b in (0, which)]
        mixed = dot(jnp.concatenate(parts, axis=1), jnp.concatenate(by_head, axis=0))
        return mixed[:, :width] / mixed[:, width:]

    out_a = attend(0, tail, 1)
    out_b = attend(heads * tail, margin, 2)
    attended = (gates * jnp.concatenate([out_a, out_b], axis=0)).astype(BF16)
    wo_copy.wait()
    new_atoms = (x_own.astype(F32) + dot(attended, wo[...])).astype(BF16)
    atoms_out[...] = new_atoms
    lifted = jnp.maximum(dot(new_atoms, wa_pad[...]), 0.0).astype(BF16)
    means = (dot(member, lifted) * inverse)[:tok_dev].astype(BF16)
    for c in range(n_col):
        tok_send[c] = means[:, c * width : c * width + share]

    def tok_copy(other):
        return pltpu.make_async_remote_copy(
            src_ref=tok_send.at[other],
            dst_ref=tok_recv.at[col],
            send_sem=tok_ssem,
            recv_sem=tok_rsem,
            device_id=(row, other),
            device_id_type=MESH,
        )

    for s in range(n_col - 1):
        tok_copy(nth(s)).start()
    tok_recv[col] = tok_send[col]
    others = pl.ds(0, n_col - 1)
    all_tokens = pltpu.make_async_remote_copy(
        src_ref=tok_send.at[others],
        dst_ref=tok_recv.at[others],
        send_sem=tok_ssem,
        recv_sem=tok_rsem,
        device_id=(row, (col + 1) % n_col),
        device_id_type=MESH,
    )
    all_tokens.wait_recv()

    all_tokens.wait_send()

    @pl.when(is_holder)
    def _():
        pltpu.make_async_remote_copy(
            src_ref=tsend.at[others],
            dst_ref=tsend.at[others],
            send_sem=table_send,
            recv_sem=table_recv,
            device_id=(row, (col + 1) % n_col),
            device_id_type=MESH,
        ).wait_send()

    @pl.when(corner_away)
    def _():
        corner_send_copy().wait_send()

    @pl.when(has_left)
    def _():
        for copy in to_left:
            copy.wait_send()

    @pl.when(has_right)
    def _():
        for copy in to_right:
            copy.wait_send()


def finish(atoms_ref, gathered, atoms_out, token_out, token_v, sems):
    atoms_copy = pltpu.make_async_copy(atoms_ref, atoms_out, sems.at[0])
    atoms_copy.start()
    rows = jnp.concatenate(
        [gathered[c].astype(F32) for c in range(gathered.shape[0])], axis=0
    )
    token_v[...] = rows.astype(BF16)
    token_copy = pltpu.make_async_copy(token_v, token_out, sems.at[1])
    token_copy.start()
    atoms_copy.wait()
    token_copy.wait()


def per_device(n_row, n_col, *args):
    x, pair, w_pair, w_query, w_keyval, w_gate, w_out, w_agg, tok, shift, mask = args
    w_pair = w_pair.T
    atoms, width = x.shape
    tok_rows, tok_cols, chan = pair.shape
    heads = w_pair.shape[0]
    tok_dev = tok_rows // n_col
    half_t = tok_dev // 2
    ct = w_agg.shape[1]
    margin = KW // 2
    lanes = -(-half_t * WIDE // 128) * 128
    hbm = pl.BlockSpec(memory_space=pltpu.HBM)
    vmem = pl.BlockSpec(memory_space=pltpu.VMEM)
    dma = pltpu.SemaphoreType.DMA
    scratch = [
        pltpu.VMEM((3 * width, width), BF16),
        pltpu.VMEM((n_col, half_t, 2 * WIDE, chan), BF16),
        pltpu.VMEM((half_t, 2 * WIDE, chan), BF16),
        pltpu.VMEM(w_pair.shape, BF16),
        pltpu.VMEM(w_query.shape, BF16),
        pltpu.VMEM(w_keyval.shape, BF16),
        pltpu.VMEM(w_gate.shape, BF16),
        pltpu.VMEM(w_out.shape, BF16),
        pltpu.VMEM(w_agg.shape, BF16),
        pltpu.VMEM((width, n_col * width), BF16),
        pltpu.VMEM(tok.shape, jnp.int32),
        pltpu.VMEM(mask.shape, jnp.int32),
        pltpu.SMEM(shift.shape, jnp.int32),
        pltpu.VMEM((n_col, 2 * heads, lanes), F32),
        pltpu.VMEM((2 * heads, lanes), F32),
        pltpu.VMEM((2 * heads, lanes), F32),
        pltpu.VMEM((2 * heads, lanes), F32),
        pltpu.VMEM((2, 8, width), jnp.int32),
        pltpu.VMEM((3, 8, width), jnp.int32),
        pltpu.VMEM((heads * atoms, 2 * width), BF16),
        pltpu.VMEM((3, 4 * width, width), BF16),
        pltpu.VMEM((3, heads, width, 2 * width), BF16),
        pltpu.VMEM((n_col, tok_dev, ct // n_col), BF16),
        dma((11,)),
        dma((n_col, 2)),
        dma((2,)),
        dma((4,)),
        dma((4,)),
        dma,
        dma,
        dma,
        dma,
        dma,
        dma,
    ]
    inputs = (x, pair, w_pair, w_query, w_keyval, w_gate, w_out, w_agg, tok, shift, mask)
    inputs = [pltpu.with_memory_space_constraint(a, pltpu.HBM) for a in inputs]
    new_atoms, gathered = pl.pallas_call(
        functools.partial(kernel, n_row, n_col),
        out_shape=(
            pltpu.VMEM((atoms, width), BF16),
            pltpu.VMEM((n_col, tok_dev, ct // n_col), BF16),
        ),
        in_specs=[hbm] * 11,
        out_specs=(vmem, vmem),
        scratch_shapes=scratch,
        compiler_params=pltpu.CompilerParams(
            collective_id=0, has_side_effects=True, vmem_limit_bytes=40 * 1024 * 1024
        ),
        name="atom_block",
    )(*inputs)
    return pl.pallas_call(
        finish,
        out_shape=(
            pltpu.HBM((atoms, width), BF16),
            pltpu.HBM((tok_rows, ct // n_col), BF16),
        ),
        in_specs=[vmem, vmem],
        out_specs=(hbm, hbm),
        scratch_shapes=[pltpu.VMEM((tok_rows, ct // n_col), BF16), dma((2,))],
        compiler_params=pltpu.CompilerParams(vmem_limit_bytes=8 * 1024 * 1024),
        name="write_out",
    )(new_atoms, gathered)


def solution(mesh):
    n_row, n_col = mesh.shape["row"], mesh.shape["col"]
    split = P(("row", "col"))
    in_specs = (
        P(("row", "col"), None),
        P("row", "col", None),
        P(),
        P(),
        P(),
        P(),
        P(),
        P(),
        split,
        split,
        split,
    )
    out_specs = (P(("row", "col"), None), P("row", "col"))
    return jax.shard_map(
        functools.partial(per_device, n_row, n_col),
        mesh=mesh,
        in_specs=in_specs,
        out_specs=out_specs,
        check_vma=False,
    )
```
